256 devices in a mesh: orient: 32 (over z, x), dom: 2 (over core), shell: 4 (over y).
Axes of the slice: x: 4, y: 4, z: 8, core: 2. Of those that a mesh axis runs over, the one named last changes fastest.
Arguments:
- references: bfloat16 [16384, 2, 4096], P('orient', None, 'shell'), may hold values from -6 to 6
- images: bfloat16 [4096, 2, 4096], P(('orient', 'dom'), None, 'shell'), may hold values from -20 to 20
- noise_var: float32 [64], replicated, may hold values from 32 to 128
- shell_of: int32 [4096], P('shell'), may hold values from 0 to 63, never falling along the last dimension, each value on 1 to 128 neighbouring positions
- kept_blocks: int32 [32, 2, 24], P('orient', 'dom'), may hold values from -1 to 31, as said below
Outputs:
- weighted: float32 [16384, 2, 4096], P(('orient', 'dom'), None, 'shell')
- log_norm: float32 [4096], P(('orient', 'dom'))
The draws below stay inside these ranges and needn't reach their ends.
Inputs may be any that keep to these rules, and one draw needn't show every extreme that they name: `kept_blocks`: each list holds distinct block numbers first, then -1 entries; the list of orientation block o and group d always starts with o; some list holds 24 blocks.
All inputs are finite; a program needn't handle non-finite values.
Results may differ from the reference program's by a relative error of at most 0.0051.
Values may be sent and summed in bfloat16 or wider, within the bound.
No kernel may reach another device: no remote copies, remote signals or barrier semaphores. Data moves between devices by JAX's collectives and lax.ppermute only.
A program may use at most 64 MiB of HBM per device.

```python
import math
import jax
import jax.numpy as jnp
import numpy as np
from jax import lax

K = 4096
SHELLS = 64
OR_DEV = 512
IMG_DEV = 64
SHELL_MOST = 128
OBLK = 32
GROUPS = 2
MOST = 24
ORIENT = 16384
IMAGES = 4096


def reference_values(key):
    base_key = jax.random.fold_in(key, 101)
    second = jax.random.fold_in(base_key, 1)
    values = jax.random.normal(second, (ORIENT, 2, K))
    return jnp.clip(values, -6.0, 6.0)


def draw_references(key, part):
    return reference_values(key).astype(jnp.bfloat16)


def draw_images(key, part):
    image_key = jax.random.fold_in(key, 202)
    second = jax.random.fold_in(image_key, 1)
    values = jax.random.normal(second, (IMAGES, 2, K))
    return jnp.clip(values, -20.0, 20.0).astype(jnp.bfloat16)


def draw_kept_blocks(key, part):
    list_key = jax.random.fold_in(key, 303)
    first, second, third = jax.random.split(list_key, 3)
    ranks = jax.random.randint(first, (OBLK, GROUPS, OBLK), 0, 1 << 20) * OBLK + jnp.arange(OBLK, dtype=jnp.int32)[None, None, :]
    itself = jnp.arange(OBLK, dtype=jnp.int32)[:, None, None] == jnp.arange(OBLK, dtype=jnp.int32)[None, None, :]
    ranks = jnp.where(itself, -1, ranks)
    order = jnp.argsort(ranks, axis=-1, stable=True)[:, :, :MOST].astype(jnp.int32)
    counts = jax.random.randint(second, (OBLK, GROUPS), 1, MOST + 1)
    chosen_row = jax.random.randint(third, (), 0, OBLK * GROUPS)
    counts = jnp.where(jnp.arange(OBLK * GROUPS, dtype=jnp.int32).reshape(OBLK, GROUPS) == chosen_row, MOST, counts)
    places = jnp.arange(MOST, dtype=jnp.int32)
    return jnp.where(places[None, None, :] < counts[:, :, None], order, -1).astype(jnp.int32)


def split_up(number_of, total, limit, lean):
    weights = [(1 << 20) // math.isqrt(rank ** lean) + 1 for rank in range(2, number_of + 1)]
    rest, given = total - limit - (number_of - 1), [1] * (number_of - 1)
    while rest > 0:
        free = [i for i in range(number_of - 1) if given[i] < limit]
        whole, budget = sum([weights[i] for i in free]), rest
        for i in free:
            more = min(limit - given[i], max(1, budget * weights[i] // whole), rest)
            given[i] = given[i] + more
            rest = rest - more
    return np.array([limit] + given)


def uneven_parts(key, amount, total, limit, skew):
    if amount == 2:
        one = jax.random.randint(key, (), max(1, total - limit), min(limit, total - 1) + 1)
        return jnp.stack([one, total - one])
    sizes = jnp.asarray(split_up(amount, total, limit, skew), jnp.int32)
    pairs = (amount - 1) // 2
    donor, taker = sizes[1:1 + 2 * pairs:2], sizes[2:2 + 2 * pairs:2]
    slack = jnp.minimum(donor - 1, limit - taker)
    passed = jax.random.randint(jax.random.fold_in(key, 1), (pairs,), 0, 1 << 20) % (slack + 1)
    sizes = sizes.at[1:1 + 2 * pairs:2].set(donor - passed).at[2:2 + 2 * pairs:2].set(taker + passed)
    return sizes[jax.random.permutation(jax.random.fold_in(key, 2), amount)]


def setup_inputs(seed: int = 0) -> dict:
    keys = jax.random.split(jax.random.key(seed), 6)
    return {
        "references": draw_references(jax.random.fold_in(keys[5], 71), 0),
        "images": draw_images(jax.random.fold_in(keys[5], 71), 0),
        "noise_var": jnp.clip(jnp.exp(jax.random.uniform(keys[2], (SHELLS,), jnp.float32, math.log(32.0), math.log(128.0))), 32.0, 128.0),
        "shell_of": jnp.searchsorted(jnp.cumsum(uneven_parts(keys[3], SHELLS, K, SHELL_MOST, 1)), jnp.arange(K), side="right").astype(jnp.int32),
        "kept_blocks": draw_kept_blocks(jax.random.fold_in(keys[5], 71), 0),
    }


floor_value = -1e30


def reference(references, images, noise_var, shell_of, kept_blocks):
    blocks = kept_blocks.shape[0]
    groups = kept_blocks.shape[1]
    coef_weight = 1.0 / noise_var[shell_of]
    scaled = (images.astype(jnp.float32) * coef_weight).astype(jnp.bfloat16)
    scaled_flat = scaled.reshape(IMAGES, 2 * K)
    both_weight = jnp.concatenate([coef_weight, coef_weight])
    found = jnp.any(kept_blocks[:, :, :, None] == jnp.arange(blocks, dtype=jnp.int32)[None, None, None, :], axis=2)
    keep_image = jnp.repeat(jnp.transpose(found, (0, 2, 1)).reshape(blocks, blocks * groups), IMG_DEV, axis=1)
    ref_blocks = references.reshape(blocks, OR_DEV, 2 * K)

    def block_scores(inputs):
        ref_rows, keep_row = inputs
        cross = lax.dot_general(ref_rows, scaled_flat, (((1,), (1,)), ((), ())), preferred_element_type=jnp.float32)
        ref_norm = jnp.sum(both_weight[None, :] * jnp.square(ref_rows.astype(jnp.float32)), axis=1)
        value = cross - 0.5 * ref_norm[:, None]
        return jnp.where(keep_row[None, :], value, floor_value)

    scores = lax.map(block_scores, (ref_blocks, keep_image))
    keep_full = keep_image[:, None, :]
    highest = jnp.max(scores, axis=(0, 1))
    total_mass = jnp.sum(jnp.where(keep_full, jnp.exp(scores - highest[None, None, :]), 0.0), axis=(0, 1))
    log_norm = highest + jnp.log(total_mass)
    posterior = jnp.where(keep_full, jnp.exp(scores - log_norm[None, None, :]), 0.0).astype(jnp.bfloat16)
    images_flat = images.reshape(IMAGES, 2 * K)

    def block_sums(post_rows):
        return jnp.dot(post_rows, images_flat, preferred_element_type=jnp.float32)

    weighted = lax.map(block_sums, posterior).reshape(ORIENT, 2, K)
    return weighted, log_norm
```

```python
import jax
import jax.numpy as jnp
from jax import lax
from jax.experimental import pallas as pl
from jax.experimental.pallas import tpu as pltpu
from jax.sharding import Mesh
from jax.sharding import PartitionSpec as P

floor_value = -1e30

NZ, NX, NY = 8, 4, 4
BLOCKS = NZ * NX
ROWS = 64
HALF = 32
MOST = 24
REFS = 512
COLS = 2048
QUARTER = MOST * 8

ORDER_A = [[(dz, dx) for dx in range(4)] for dz in (0, 7, 1, 6, 2, 5, 3)] + [
    [(4, 0), (4, 1)],
    [(4, 2), (4, 3)],
]
ORDER_B = [[(dz, dx) for dz in range(8)] for dx in (0, 3, 1)] + [
    [(dz, 2) for dz in range(4)],
    [(dz, 2) for dz in range(4, 8)],
]
VMEM = pl.BlockSpec(memory_space=pltpu.VMEM)
SMEM = pl.BlockSpec(memory_space=pltpu.SMEM)


def step(value, axis, count, by):
    return lax.ppermute(value, axis, [(i, (i + by) % count) for i in range(count)])


def gather_first(half):
    low = step(half, "x", NX, 1)
    high = step(half, "x", NX, -1)
    far_top = step(low[:16], "x", NX, 1)
    far_bottom = step(high[16:], "x", NX, -1)
    mine = jnp.concatenate([half, high, far_top, far_bottom, low])
    pieces = [mine]
    down, up = mine, mine
    for _ in range(3):
        down = step(down, "z", NZ, 1)
        up = step(up, "z", NZ, -1)
        pieces += [down, up]
    return pieces + [step(down[:64], "z", NZ, 1), step(up[64:], "z", NZ, -1)]


def gather_second(half):
    downs, ups = [half], [half]
    for _ in range(3):
        downs.append(step(downs[-1], "z", NZ, 1))
        ups.append(step(ups[-1], "z", NZ, -1))
    far = [step(downs[3][:16], "z", NZ, 1), step(ups[3][16:], "z", NZ, -1)]
    mine = jnp.concatenate(ups + far + downs[:0:-1])
    low = step(mine, "x", NX, 1)
    high = step(mine, "x", NX, -1)
    return [mine, low, high, step(low[:128], "x", NX, 1), step(high[128:], "x", NX, -1)]


def scores_kernel(order, tab, refs, weight, norm, *rest):
    arrays, (keep0, keep1, send, held) = rest[: len(order)], rest[len(order) :]
    targets = [(keep0, 0), (keep1, 0), (send, 0), (send, QUARTER)]
    at = 0
    for blocks, piece in zip(order, arrays):
        scaled = (piece[...].astype(jnp.float32) * weight[...]).astype(jnp.bfloat16)
        held[: piece.shape[0], :] = (
            jnp.dot(scaled, refs[...], preferred_element_type=jnp.float32) - norm[...]
        )
        for i in range(len(blocks)):
            slot = tab[at]
            at += 1

            @pl.when(slot >= 0)
            def _(slot=slot, i=i):
                for t, (out, base) in enumerate(targets):
                    row = pl.multiple_of(tab[BLOCKS + t] * 8, 8) + i * HALF
                    out[pl.ds(pl.multiple_of(slot * 8, 8) + base, 8), :] = held[pl.ds(row, 8), :]


def partial_scores(order, tab, refs, weight, norm, pieces):
    part = jax.ShapeDtypeStruct((QUARTER, REFS), jnp.float32)
    both = jax.ShapeDtypeStruct((2 * QUARTER, REFS), jnp.float32)
    most = max(p.shape[0] for p in pieces)
    return pl.pallas_call(
        lambda *refs_: scores_kernel(order, *refs_),
        out_shape=(part, part, both),
        in_specs=[SMEM] + [VMEM] * (3 + len(pieces)),
        out_specs=(VMEM, VMEM, VMEM),
        scratch_shapes=[pltpu.VMEM((most, REFS), jnp.float32)],
        compiler_params=pltpu.CompilerParams(vmem_limit_bytes=40 << 20),
        cost_estimate=pl.CostEstimate(
            flops=2 * 1024 * COLS * REFS, bytes_accessed=8 << 20, transcendentals=0
        ),
        name="partial_scores",
    )(tab, refs, weight, norm, *pieces)


def diagonal():
    return lax.broadcasted_iota(jnp.int32, (128, 128), 0) == lax.broadcasted_iota(
        jnp.int32, (128, 128), 1
    )


def local_kernel(kept, a0, a1, a2, b0, b1, b2, probs, stats, high, mass):
    high[...] = jnp.full(high.shape, floor_value, jnp.float32)
    mass[...] = jnp.zeros(mass.shape, jnp.float32)
    parts = []
    for first, second, third in ((a0, a1, a2), (b0, b1, b2)):
        score = first[...] + second[:QUARTER, :] + third[...]
        top = jnp.max(score, axis=1, keepdims=True)
        value = jnp.exp(score - top)
        parts.append((top, value, jnp.sum(value, axis=1, keepdims=True)))
    for j in range(MOST):
        block = kept[j]
        valid = block >= 0
        rows = slice(8 * j, 8 * j + 8)
        both = jnp.concatenate([value[rows] for _, value, _ in parts], axis=0)
        probs[16 * j : 16 * j + 16, :] = jnp.where(valid, both, 0.0).astype(jnp.bfloat16)

        @pl.when(valid)
        def _(block=block, rows=rows):
            for k, (top, _, total) in enumerate(parts):
                at = pl.ds(pl.multiple_of(block * 8, 8) + k * 256, 8)
                high[at, :] = jnp.broadcast_to(top[rows], (8, 128))
                mass[at, :] = jnp.broadcast_to(total[rows], (8, 128))

    eye = diagonal()
    for k, source in enumerate((high, mass)):
        for g in range(4):
            square = source[128 * g : 128 * g + 128, :]
            stats[4 * k + g : 4 * k + g + 1, :] = jnp.sum(
                jnp.where(eye, square, 0.0), axis=0, keepdims=True
            )


def local_stats(kept, a, b):
    return pl.pallas_call(
        local_kernel,
        out_shape=(
            jax.ShapeDtypeStruct((MOST * 16, REFS), jnp.bfloat16),
            jax.ShapeDtypeStruct((8, 128), jnp.float32),
        ),
        in_specs=[SMEM] + [VMEM] * 6,
        out_specs=(VMEM, VMEM),
        scratch_shapes=[pltpu.VMEM((512, 128), jnp.float32)] * 2,
        compiler_params=pltpu.CompilerParams(vmem_limit_bytes=30 << 20),
        name="local_stats",
    )(kept, *a, *b)


def combine_kernel(everyone, own, out):
    highs, masses = everyone[:, 0:4, :], everyone[:, 4:8, :]
    top = jnp.max(highs, axis=0)
    total = jnp.sum(masses * jnp.exp(highs - top[None]), axis=0)
    log_norm = top + jnp.log(total)
    out[0:4, :] = jnp.exp(own[0:4, :] - log_norm)
    out[4:8, :] = log_norm


def combine(everyone, own):
    return pl.pallas_call(
        combine_kernel,
        out_shape=jax.ShapeDtypeStruct((8, 128), jnp.float32),
        in_specs=[VMEM, VMEM],
        out_specs=VMEM,
        name="combine_stats",
    )(everyone, own)


def product(out, flipped, base, arrays):
    rows = pl.ds(pl.multiple_of(base, 256), 256)
    for c in range(0, COLS, 512):
        total = jnp.zeros((256, 512), jnp.float32)
        at = 0
        for piece in arrays:
            n = piece.shape[0]
            total += jnp.dot(
                flipped[rows, at : at + n],
                piece[:, c : c + 512],
                preferred_element_type=jnp.float32,
            )
            at += n
        out[:, c : c + 512] = total


def send_kernel(tab, scale, probs, *rest):
    arrays, (out, flipped, column, dense) = rest[:-4], rest[-4:]
    eye = diagonal()
    for q in range(NY):
        for g in range(4):
            spread = jnp.broadcast_to(scale[q, g : g + 1, :], (128, 128))
            one = jnp.sum(jnp.where(eye, spread, 0.0), axis=1, keepdims=True)
            column[q, 128 * g : 128 * g + 128, :] = jnp.broadcast_to(one, (128, 128))
    for k in range(2):

        def fill(n, carry, k=k):
            slot = tab[2 * k * BLOCKS + n]
            block = tab[(2 * k + 1) * BLOCKS + n]
            at = pl.multiple_of(jnp.maximum(slot, 0) * 16, 16)
            parts = []
            for q in range(NY):
                source = tab[4 * BLOCKS + 2 + q]
                value = probs[source, pl.ds(at, 16), :].astype(jnp.float32)[8 * k : 8 * k + 8]
                factor = column[q, pl.ds(pl.multiple_of(block * 8, 8) + 256 * k, 8), :]
                parts.append(value * jnp.concatenate([factor] * 4, axis=1))
            rows = jnp.where(slot >= 0, jnp.concatenate(parts, axis=0), 0.0)
            dense[pl.ds(pl.multiple_of(n * HALF, HALF), HALF), :] = rows.astype(jnp.bfloat16)
            return carry

        lax.fori_loop(0, BLOCKS, fill, 0)
        flipped[:, 1024 * k : 1024 * k + 1024] = dense[...].T
    product(out, flipped, tab[4 * BLOCKS], arrays)


def keep_kernel(tab, flipped, *rest):
    product(rest[-1], flipped, tab[4 * BLOCKS + 1], rest[:-1])


def weighted_sums(tab, scale, probs, pieces):
    half = jax.ShapeDtypeStruct((REFS // 2, COLS), jnp.float32)
    cost = pl.CostEstimate(
        flops=2 * 2048 * COLS * REFS // 2, bytes_accessed=12 << 20, transcendentals=0
    )
    out, flipped = pl.pallas_call(
        send_kernel,
        out_shape=(half, jax.ShapeDtypeStruct((REFS, COLS), jnp.bfloat16)),
        in_specs=[SMEM] + [VMEM] * (2 + len(pieces)),
        out_specs=(VMEM, VMEM),
        scratch_shapes=[
            pltpu.VMEM((NY, 512, 128), jnp.float32),
            pltpu.VMEM((1024, REFS), jnp.bfloat16),
        ],
        compiler_params=pltpu.CompilerParams(vmem_limit_bytes=45 << 20),
        cost_estimate=cost,
        name="weighted_send",
    )(tab, scale, probs, *pieces)
    other = lax.ppermute(out, "dom", [(0, 1), (1, 0)])
    mine = pl.pallas_call(
        keep_kernel,
        out_shape=half,
        in_specs=[SMEM] + [VMEM] * (1 + len(pieces)),
        out_specs=VMEM,
        compiler_params=pltpu.CompilerParams(vmem_limit_bytes=45 << 20),
        cost_estimate=cost,
        name="weighted_keep",
    )(tab, flipped, *pieces)
    return mine + other


def shards(references, images, noise_var, shell_of, kept_blocks):
    z, x = lax.axis_index("z"), lax.axis_index("x")
    d, y = lax.axis_index("dom"), lax.axis_index("shell")
    kept = kept_blocks.reshape(MOST)

    img = images.reshape(ROWS, COLS)
    pieces_a = gather_first(img[:HALF])
    pieces_b = gather_second(img[HALF:])

    shells = jnp.arange(noise_var.shape[0], dtype=jnp.int32)
    picked = jnp.where(shells[:, None] == shell_of[None, :], noise_var[:, None], 0.0)
    weight = 1.0 / jnp.sum(picked, axis=0)
    weight = jnp.concatenate([weight, weight])
    flat = references.reshape(REFS, COLS)
    norm = 0.5 * jnp.sum(weight * jnp.square(flat.astype(jnp.float32)), axis=1)[None, :]
    weight = weight[None, :]
    refs = flat.T

    def places(order):
        offsets = jnp.array([b for piece in order for b in piece], jnp.int32)
        block = ((z + offsets[:, 0]) % NZ) * NX + (x + offsets[:, 1]) % NX
        hit = kept[None, :] == block[:, None]
        slots = jnp.arange(MOST, dtype=jnp.int32)[None, :]
        return jnp.max(jnp.where(hit, slots, -1), axis=1), block

    slot_a, block_a = places(ORDER_A)
    slot_b, block_b = places(ORDER_B)
    near, far = y ^ 1, 3 - y
    quarters_a = jnp.stack([y, far, near, 3 - near])
    quarters_b = jnp.stack([y, near, far, far ^ 1])
    to_near = [(0, 1), (1, 0), (2, 3), (3, 2)]
    to_far = [(0, 3), (3, 0), (1, 2), (2, 1)]

    def summed(order, slot, quarters, pieces, first, second):
        keep0, keep1, send = partial_scores(
            order, jnp.concatenate([slot, quarters]), refs, weight, norm, pieces
        )
        got = lax.ppermute(send, "shell", first)
        last = lax.ppermute(keep1 + got[QUARTER:], "shell", second)
        return keep0, got, last

    sum_a = summed(ORDER_A, slot_a, quarters_a, pieces_a, to_near, to_far)
    sum_b = summed(ORDER_B, slot_b, quarters_b, pieces_b, to_far, to_near)

    probs, stats = local_stats(kept, sum_a, sum_b)

    cut = MOST * 8
    top1 = lax.ppermute(probs[:cut], "shell", to_far)
    low1 = lax.ppermute(probs[cut:], "shell", to_near)
    top2 = lax.ppermute(jnp.stack([probs[:cut], top1]), "shell", to_near)
    low2 = lax.ppermute(jnp.stack([probs[cut:], low1]), "shell", to_far)
    everyone = lax.all_to_all(
        jnp.broadcast_to(stats[None], (BLOCKS, 8, 128)), ("z", "x"), 0, 0, tiled=True
    )
    scale = lax.all_to_all(
        jnp.broadcast_to(combine(everyone, stats)[None], (NY, 8, 128)), "shell", 0, 0, tiled=True
    )
    tops = jnp.concatenate([probs[None, :cut], top1[None], top2])
    lows = jnp.concatenate([probs[None, cut:], low1[None], low2])
    own = jnp.concatenate([tops, jnp.stack([lows[0], lows[2], lows[1], lows[3]])], axis=1)
    order = jnp.stack([y, far, near, 3 - near])
    ranks = jnp.arange(NY, dtype=jnp.int32)
    source = jnp.sum(jnp.where(order[None, :] == ranks[:, None], ranks[None, :], 0), axis=1)

    tab = jnp.concatenate(
        [slot_a, block_a, slot_b, block_b, jnp.stack([(1 - d) * 256, d * 256]), source]
    ).astype(jnp.int32)
    weighted = weighted_sums(tab, scale, own, pieces_a + pieces_b)

    home = z * NX + x
    log_norms = scale[:, 4:8, :].reshape(NY, 2, BLOCKS, 8)
    here = jnp.arange(BLOCKS, dtype=jnp.int32) == home
    log_norm = jnp.sum(jnp.where(here[None, None, :, None], log_norms, 0.0), axis=2)
    log_norm = jnp.transpose(log_norm, (1, 0, 2)).reshape(ROWS)
    return weighted.reshape(REFS // 2, 2, COLS // 2), log_norm


def solution(mesh):
    wide = Mesh(mesh.devices.reshape(NZ, NX, 2, NY), ("z", "x", "dom", "shell"))
    orient = ("z", "x")
    placed = (
        P(orient, None, "shell"),
        P(("z", "x", "dom"), None, "shell"),
        P(),
        P("shell"),
        P(orient, "dom", None),
    )
    return jax.shard_map(
        shards,
        mesh=wide,
        in_specs=placed,
        out_specs=(P(("z", "x", "dom"), None, "shell"), P(("z", "x", "dom"))),
        check_vma=False,
    )
```

```python
import jax
import jax.numpy as jnp
from jax import lax
from jax.experimental import pallas as pl
from jax.experimental.pallas import tpu as pltpu
from jax.sharding import Mesh
from jax.sharding import PartitionSpec as P

floor_value = -1e30

NZ, NX, NY = 8, 4, 4
BLOCKS = NZ * NX
ROWS = 64
HALF = 32
MOST = 24
REFS = 512
COLS = 2048
QUARTER = MOST * 8

ORDER_A = [[(dz, dx) for dx in range(4)] for dz in (0, 7, 1, 6, 2, 5, 3)] + [
    [(4, 0), (4, 1)],
    [(4, 2), (4, 3)],
]
ORDER_B = [[(dz, dx) for dz in range(8)] for dx in (0, 3, 1)] + [
    [(dz, 2) for dz in range(4)],
    [(dz, 2) for dz in range(4, 8)],
]
VMEM = pl.BlockSpec(memory_space=pltpu.VMEM)
SMEM = pl.BlockSpec(memory_space=pltpu.SMEM)
ANY = pl.BlockSpec(memory_space=pl.ANY)


def step(value, axis, count, by):
    return lax.ppermute(value, axis, [(i, (i + by) % count) for i in range(count)])


def fetch(arrays, whole, sems, first=0):
    copies, base = [], 0
    for i, piece in enumerate(arrays):
        rows = piece.shape[0]
        copy = pltpu.make_async_copy(
            piece, whole.at[pl.ds(base, rows), :], sems.at[first + i]
        )
        copy.start()
        copies.append((copy, base, rows))
        base += rows
    return copies


def join_kernel(*rest):
    arrays, (out, sems) = rest[:-2], rest[-2:]
    for copy, _, _ in fetch(arrays, out, sems):
        copy.wait()


def joined(arrays):
    rows = sum(a.shape[0] for a in arrays)
    return pl.pallas_call(
        join_kernel,
        out_shape=jax.ShapeDtypeStruct((rows, COLS), jnp.bfloat16),
        in_specs=[ANY] * len(arrays),
        out_specs=ANY,
        scratch_shapes=[pltpu.SemaphoreType.DMA((len(arrays),))],
        compiler_params=pltpu.CompilerParams(vmem_limit_bytes=1 << 20),
        cost_estimate=pl.CostEstimate(
            flops=0, bytes_accessed=2 * rows * COLS, transcendentals=0
        ),
        name="joined",
    )(*arrays)


def halves_kernel(first, second, top, low):
    rows = top.shape[0]
    top[...] = first[:rows, :]
    low[...] = second[rows:, :]


def halves(first, second):
    rows, wide = first.shape
    half = jax.ShapeDtypeStruct((rows // 2, wide), first.dtype)
    return pl.pallas_call(
        halves_kernel,
        out_shape=(half, half),
        in_specs=[VMEM] * 2,
        out_specs=(VMEM, VMEM),
        compiler_params=pltpu.CompilerParams(vmem_limit_bytes=1 << 20),
        name="halves",
    )(first, second)


def both_ways(up, down, axis, count):
    return step(up, axis, count, 1), step(down, axis, count, -1)


def gather(half_a, half_b, flat, norm_of, tables):
    low, high = both_ways(half_a, half_a, "x", NX)
    downs, ups = [half_b], [half_b]
    for _ in range(2):
        down, up = both_ways(downs[-1], ups[-1], "z", NZ)
        downs.append(down)
        ups.append(up)
    far_top, far_bottom = both_ways(*halves(low, high), "x", NX)
    down, up = both_ways(downs[-1], ups[-1], "z", NZ)
    downs.append(down)
    ups.append(up)
    far = both_ways(*halves(down, up), "z", NZ)
    mine_a = joined([half_a, high, far_top, far_bottom, low])
    mine_b = joined([*ups, *far, *downs[:0:-1]])
    mine_a, mine_b, tables = lax.optimization_barrier((mine_a, mine_b, tables))

    down, up = both_ways(mine_a, mine_a, "z", NZ)
    low, high = both_ways(mine_b, mine_b, "x", NX)
    pieces_a = [mine_a, down, up]
    down, up, flat = lax.optimization_barrier((down, up, flat))
    down, up = both_ways(down, up, "z", NZ)
    pieces_a += [down, up]
    norm = norm_of(flat)
    down, up, norm = lax.optimization_barrier((down, up, norm))
    far_b = both_ways(*halves(low, high), "x", NX)
    down, up = both_ways(down, up, "z", NZ)
    pieces_a += [down, up]
    pieces_a += both_ways(*halves(down, up), "z", NZ)
    return pieces_a, [mine_b, low, high, *far_b], flat, norm, tables


def scores_kernel(order, tab, refs, weight, norm, *rest):
    arrays = rest[: len(order)]
    outs, (parts, whole, scaled, held, near_refs, sems) = (
        rest[len(order) : len(order) + 3],
        rest[len(order) + 3 :],
    )
    copies = fetch(arrays, whole, sems)
    [(refs_copy, _, _)] = fetch([refs], near_refs, sems, len(order))
    for copy, base, count in copies:
        copy.wait()

        def tile(i, carry, base=base):
            rows = pl.ds(pl.multiple_of(base + i * 16, 16), 16)
            scaled[rows, :] = (whole[rows, :].astype(jnp.float32) * weight[...]).astype(
                jnp.bfloat16
            )
            return carry

        lax.fori_loop(0, count // 16, tile, 0)
    refs_copy.wait()
    held[...] = (
        lax.dot_general(
            scaled[...],
            near_refs[...],
            (((1,), (1,)), ((), ())),
            preferred_element_type=jnp.float32,
        )
        - norm[...]
    )
    for n in range(BLOCKS):
        slot = tab[n]

        @pl.when(slot >= 0)
        def _(slot=slot, n=n):
            for t in range(NY):
                row = pl.multiple_of(tab[BLOCKS + t] * 8, 8) + n * HALF
                to = pl.ds(pl.multiple_of(slot * 8, 8) + t * QUARTER, 8)
                parts[to, :] = held[pl.ds(row, 8), :]

    done = []
    for i, (out, t, count) in enumerate(zip(outs, (2, 0, 1), (2, 1, 1))):
        source = parts.at[pl.ds(t * QUARTER, count * QUARTER), :]
        done.append(pltpu.make_async_copy(source, out, sems.at[len(order) + 1 + i]))
        done[-1].start()
    for copy in done:
        copy.wait()


def partial_scores(order, tab, refs, weight, norm, pieces):
    part = jax.ShapeDtypeStruct((QUARTER, REFS), jnp.float32)
    both = jax.ShapeDtypeStruct((2 * QUARTER, REFS), jnp.float32)
    return pl.pallas_call(
        lambda *refs_: scores_kernel(order, *refs_),
        out_shape=(both, part, part),
        in_specs=[SMEM, ANY, VMEM, VMEM] + [ANY] * len(pieces),
        out_specs=(ANY, ANY, ANY),
        scratch_shapes=[
            pltpu.VMEM((NY * QUARTER, REFS), jnp.float32),
            pltpu.VMEM((1024, COLS), jnp.bfloat16),
            pltpu.VMEM((1024, COLS), jnp.bfloat16),
            pltpu.VMEM((1024, REFS), jnp.float32),
            pltpu.VMEM((REFS, COLS), jnp.bfloat16),
            pltpu.SemaphoreType.DMA((len(pieces) + 4,)),
        ],
        compiler_params=pltpu.CompilerParams(vmem_limit_bytes=20 << 20),
        cost_estimate=pl.CostEstimate(
            flops=2 * 1024 * COLS * REFS, bytes_accessed=8 << 20, transcendentals=0
        ),
        name="partial_scores",
    )(tab, refs, weight, norm, *pieces)


def diagonal():
    return lax.broadcasted_iota(jnp.int32, (128, 128), 0) == lax.broadcasted_iota(
        jnp.int32, (128, 128), 1
    )


def local_kernel(kept, a0, a1, a2, b0, b1, b2, probs, stats, high, mass):
    high[...] = jnp.full(high.shape, floor_value, jnp.float32)
    mass[...] = jnp.zeros(mass.shape, jnp.float32)
    parts = []
    for first, second, third in ((a0, a1, a2), (b0, b1, b2)):
        score = first[...] + second[:QUARTER, :] + third[...]
        top = jnp.max(score, axis=1, keepdims=True)
        value = jnp.exp(score - top)
        parts.append((top, value, jnp.sum(value, axis=1, keepdims=True)))
    for j in range(MOST):
        block = kept[j]
        valid = block >= 0
        rows = slice(8 * j, 8 * j + 8)
        both = jnp.concatenate([value[rows] for _, value, _ in parts], axis=0)
        probs[16 * j : 16 * j + 16, :] = jnp.where(valid, both, 0.0).astype(jnp.bfloat16)

        @pl.when(valid)
        def _(block=block, rows=rows):
            for k, (top, _, total) in enumerate(parts):
                at = pl.ds(pl.multiple_of(block * 8, 8) + k * 256, 8)
                high[at, :] = jnp.broadcast_to(top[rows], (8, 128))
                mass[at, :] = jnp.broadcast_to(total[rows], (8, 128))

    eye = diagonal()
    for k, source in enumerate((high, mass)):
        for g in range(4):
            square = source[128 * g : 128 * g + 128, :]
            row = jnp.sum(jnp.where(eye, square, 0.0), axis=0, keepdims=True)
            stats[:, 4 * k + g : 4 * k + g + 1, :] = jnp.broadcast_to(row[None], (BLOCKS, 1, 128))


def local_stats(kept, a, b):
    return pl.pallas_call(
        local_kernel,
        out_shape=(
            jax.ShapeDtypeStruct((MOST * 16, REFS), jnp.bfloat16),
            jax.ShapeDtypeStruct((BLOCKS, 8, 128), jnp.float32),
        ),
        in_specs=[SMEM] + [VMEM] * 6,
        out_specs=(VMEM, VMEM),
        scratch_shapes=[pltpu.VMEM((512, 128), jnp.float32)] * 2,
        compiler_params=pltpu.CompilerParams(vmem_limit_bytes=12 << 20),
        name="local_stats",
    )(kept, *a, *b)


def combine_kernel(everyone, own, out):
    highs, masses = everyone[:, 0:4, :], everyone[:, 4:8, :]
    top = jnp.max(highs, axis=0)
    total = jnp.sum(masses * jnp.exp(highs - top[None]), axis=0)
    log_norm = top + jnp.log(total)
    both = jnp.concatenate([jnp.exp(own[0, 0:4, :] - log_norm), log_norm], axis=0)
    out[...] = jnp.broadcast_to(both[None], out.shape)


def combine(everyone, own):
    return pl.pallas_call(
        combine_kernel,
        out_shape=jax.ShapeDtypeStruct((NY, 8, 128), jnp.float32),
        in_specs=[VMEM, VMEM],
        out_specs=VMEM,
        name="combine_stats",
    )(everyone, own)


def send_kernel(tab, scale, own, far, near, top, low, *rest):
    arrays, (out, rest_flipped) = rest[:-9], rest[-9:-7]
    total, flipped, images, column, dense, probs, sems = rest[-7:]
    copies = fetch(arrays, images, sems)
    cut = MOST * 8
    for i, source in enumerate((own, far, near)):
        probs[i] = source[...]
    probs[3, :cut, :] = top[...]
    probs[3, cut:, :] = low[...]
    eye = diagonal()
    for q in range(NY):
        for g in range(4):
            spread = jnp.broadcast_to(scale[q, g : g + 1, :], (128, 128))
            one = jnp.sum(jnp.where(eye, spread, 0.0), axis=1, keepdims=True)
            column[q, 128 * g : 128 * g + 128, :] = jnp.broadcast_to(one, (128, 128))
    for k in range(2):

        def fill(n, carry, k=k):
            slot = tab[2 * k * BLOCKS + n]
            block = tab[(2 * k + 1) * BLOCKS + n]
            at = pl.multiple_of(jnp.maximum(slot, 0) * 16, 16)
            parts = []
            for q in range(NY):
                source = tab[4 * BLOCKS + 2 + q]
                value = probs[source, pl.ds(at, 16), :].astype(jnp.float32)[8 * k : 8 * k + 8]
                factor = column[q, pl.ds(pl.multiple_of(block * 8, 8) + 256 * k, 8), :]
                parts.append(value * jnp.concatenate([factor] * 4, axis=1))
            rows = jnp.where(slot >= 0, jnp.concatenate(parts, axis=0), 0.0)
            dense[pl.ds(pl.multiple_of(n * HALF, HALF), HALF), :] = rows.astype(jnp.bfloat16)
            return carry

        lax.fori_loop(0, BLOCKS, fill, 0)
        flipped[:, 1024 * k : 1024 * k + 1024] = dense[...].T
    own_rows = pl.ds(pl.multiple_of(tab[4 * BLOCKS + 1], 256), 256)
    hand_on = pltpu.make_async_copy(flipped.at[own_rows, :], rest_flipped, sems.at[len(arrays)])
    hand_on.start()
    for copy, _, _ in copies:
        copy.wait()
    other_rows = pl.ds(pl.multiple_of(tab[4 * BLOCKS], 256), 256)
    total[...] = jnp.dot(
        flipped[other_rows, :], images[...], preferred_element_type=jnp.float32
    )
    write = pltpu.make_async_copy(total, out, sems.at[len(arrays) + 1])
    write.start()
    write.wait()
    hand_on.wait()


def keep_kernel(flipped, *rest):
    arrays, (out, near_flipped, images, sems) = rest[:-4], rest[-4:]
    own = pltpu.make_async_copy(flipped, near_flipped, sems.at[len(arrays)])
    own.start()
    copies = fetch(arrays, images, sems)
    own.wait()
    for part in range(2):
        for copy, base, _ in copies:
            if base // 1024 == part:
                copy.wait()
        span = slice(1024 * part, 1024 * part + 1024)
        value = jnp.dot(
            near_flipped[:, span], images[span, :], preferred_element_type=jnp.float32
        )
        if part == 0:
            out[...] = value
        else:
            out[...] += value


def final_kernel(mine, other, out):
    total = mine[...] + other[...]
    out[:, 0, :] = total[:, : COLS // 2]
    out[:, 1, :] = total[:, COLS // 2 :]


def weighted_sums(tab, scale, probs, pieces):
    half = jax.ShapeDtypeStruct((REFS // 2, COLS), jnp.float32)
    cost = pl.CostEstimate(
        flops=2 * 2048 * COLS * REFS // 2, bytes_accessed=12 << 20, transcendentals=0
    )
    out, flipped = pl.pallas_call(
        send_kernel,
        out_shape=(half, jax.ShapeDtypeStruct((REFS // 2, COLS), jnp.bfloat16)),
        in_specs=[SMEM] + [VMEM] * 6 + [ANY] * len(pieces),
        out_specs=(ANY, ANY),
        scratch_shapes=[
            pltpu.VMEM((REFS // 2, COLS), jnp.float32),
            pltpu.VMEM((REFS, COLS), jnp.bfloat16),
            pltpu.VMEM((2048, COLS), jnp.bfloat16),
            pltpu.VMEM((NY, 512, 128), jnp.float32),
            pltpu.VMEM((1024, REFS), jnp.bfloat16),
            pltpu.VMEM((NY, MOST * 16, REFS), jnp.bfloat16),
            pltpu.SemaphoreType.DMA((len(pieces) + 2,)),
        ],
        compiler_params=pltpu.CompilerParams(vmem_limit_bytes=60 << 20),
        cost_estimate=cost,
        name="weighted_send",
    )(tab, scale, *probs, *pieces)
    other = lax.ppermute(out, "dom", [(0, 1), (1, 0)])
    mine = pl.pallas_call(
        keep_kernel,
        out_shape=half,
        in_specs=[ANY] * (1 + len(pieces)),
        out_specs=VMEM,
        scratch_shapes=[
            pltpu.VMEM((REFS // 2, COLS), jnp.bfloat16),
            pltpu.VMEM((2048, COLS), jnp.bfloat16),
            pltpu.SemaphoreType.DMA((len(pieces) + 1,)),
        ],
        compiler_params=pltpu.CompilerParams(vmem_limit_bytes=60 << 20),
        cost_estimate=cost,
        name="weighted_keep",
    )(flipped, *pieces)
    return pl.pallas_call(
        final_kernel,
        out_shape=jax.ShapeDtypeStruct((REFS // 2, 2, COLS // 2), jnp.float32),
        in_specs=[VMEM, VMEM],
        out_specs=VMEM,
        compiler_params=pltpu.CompilerParams(vmem_limit_bytes=20 << 20),
        name="both_groups",
    )(mine, other)


def shards(references, images, noise_var, shell_of, kept_blocks):
    z, x = lax.axis_index("z"), lax.axis_index("x")
    d, y = lax.axis_index("dom"), lax.axis_index("shell")
    kept = kept_blocks.reshape(MOST)

    shells = jnp.arange(noise_var.shape[0], dtype=jnp.int32)
    picked = jnp.where(shells[:, None] == shell_of[None, :], noise_var[:, None], 0.0)
    weight = 1.0 / jnp.sum(picked, axis=0)
    weight = jnp.concatenate([weight, weight])

    def norm_of(flat):
        return 0.5 * jnp.sum(weight * jnp.square(flat.astype(jnp.float32)), axis=1)[None, :]

    def places(order):
        offsets = jnp.array([b for piece in order for b in piece], jnp.int32)
        block = ((z + offsets[:, 0]) % NZ) * NX + (x + offsets[:, 1]) % NX
        hit = kept[None, :] == block[:, None]
        slots = jnp.arange(MOST, dtype=jnp.int32)[None, :]
        return jnp.max(jnp.where(hit, slots, -1), axis=1), block

    slot_a, block_a = places(ORDER_A)
    slot_b, block_b = places(ORDER_B)
    near, far = y ^ 1, 3 - y
    quarters_a = jnp.stack([y, far, near, 3 - near])
    quarters_b = jnp.stack([y, near, far, far ^ 1])
    to_near = [(0, 1), (1, 0), (2, 3), (3, 2)]
    to_far = [(0, 3), (3, 0), (1, 2), (2, 1)]

    order = jnp.stack([y, far, near, 3 - near])
    ranks = jnp.arange(NY, dtype=jnp.int32)
    source = jnp.sum(jnp.where(order[None, :] == ranks[:, None], ranks[None, :], 0), axis=1)

    tab = jnp.concatenate(
        [slot_a, block_a, slot_b, block_b, jnp.stack([(1 - d) * 256, d * 256]), source]
    ).astype(jnp.int32)
    tab_a = jnp.concatenate([slot_a, quarters_a]).astype(jnp.int32)
    tab_b = jnp.concatenate([slot_b, quarters_b]).astype(jnp.int32)

    img = images.reshape(ROWS, COLS)
    pieces_a, pieces_b, refs, norm, (tab_a, tab_b, tab) = gather(
        img[:HALF], img[HALF:], references.reshape(REFS, COLS), norm_of, (tab_a, tab_b, tab)
    )
    weight = weight[None, :]

    def summed(order, tab, pieces, first, second):
        send, keep0, keep1 = partial_scores(
            order, tab, refs, weight, norm, pieces
        )
        got = lax.ppermute(send, "shell", first)
        last = lax.ppermute(keep1 + got[QUARTER:], "shell", second)
        return keep0, got, last

    sum_a = summed(ORDER_A, tab_a, pieces_a, to_near, to_far)
    sum_b = summed(ORDER_B, tab_b, pieces_b, to_far, to_near)

    probs, stats = local_stats(kept, sum_a, sum_b)

    from_near = lax.ppermute(probs, "shell", to_near)
    from_far = lax.ppermute(probs, "shell", to_far)
    top, low = halves(from_far, from_near)
    across_top = lax.ppermute(top, "shell", to_near)
    across_low = lax.ppermute(low, "shell", to_far)
    everyone = lax.all_to_all(
        stats, ("z", "x"), 0, 0, tiled=True
    )
    scale = lax.all_to_all(
        combine(everyone, stats), "shell", 0, 0, tiled=True
    )
    weighted = weighted_sums(tab, scale, (probs, from_far, from_near, across_top, across_low), pieces_a + pieces_b)

    home = z * NX + x
    log_norms = scale[:, 4:8, :].reshape(NY, 2, BLOCKS, 8)
    here = jnp.arange(BLOCKS, dtype=jnp.int32) == home
    log_norm = jnp.sum(jnp.where(here[None, None, :, None], log_norms, 0.0), axis=2)
    log_norm = jnp.transpose(log_norm, (1, 0, 2)).reshape(ROWS)
    return weighted, log_norm


def solution(mesh):
    wide = Mesh(mesh.devices.reshape(NZ, NX, 2, NY), ("z", "x", "dom", "shell"))
    orient = ("z", "x")
    placed = (
        P(orient, None, "shell"),
        P(("z", "x", "dom"), None, "shell"),
        P(),
        P("shell"),
        P(orient, "dom", None),
    )
    return jax.shard_map(
        shards,
        mesh=wide,
        in_specs=placed,
        out_specs=(P(("z", "x", "dom"), None, "shell"), P(("z", "x", "dom"))),
        check_vma=False,
    )
```

```python
import jax
import jax.numpy as jnp
from jax import lax
from jax.experimental import pallas as pl
from jax.experimental.pallas import tpu as pltpu
from jax.sharding import Mesh
from jax.sharding import PartitionSpec as P

floor_value = -1e30

NZ, NX, NY = 8, 4, 4
BLOCKS = NZ * NX
ROWS = 64
HALF = 32
MOST = 24
REFS = 512
COLS = 2048
QUARTER = MOST * 8

ORDER_A = [[(dz, dx) for dx in range(4)] for dz in (0, 7, 1, 6, 2, 5, 3)] + [
    [(4, 0), (4, 1)],
    [(4, 2), (4, 3)],
]
ORDER_B = [[(dz, dx) for dz in range(8)] for dx in (0, 3, 1)] + [
    [(dz, 2) for dz in range(4)],
    [(dz, 2) for dz in range(4, 8)],
]
VMEM = pl.BlockSpec(memory_space=pltpu.VMEM)
SMEM = pl.BlockSpec(memory_space=pltpu.SMEM)
ANY = pl.BlockSpec(memory_space=pl.ANY)


def step(value, axis, count, by):
    return lax.ppermute(value, axis, [(i, (i + by) % count) for i in range(count)])


def fetch(arrays, whole, sems, first=0):
    copies, base = [], 0
    for i, piece in enumerate(arrays):
        rows = piece.shape[0]
        copy = pltpu.make_async_copy(
            piece, whole.at[pl.ds(base, rows), :], sems.at[first + i]
        )
        copy.start()
        copies.append((copy, base, rows))
        base += rows
    return copies


def join_kernel(*rest):
    arrays, (out, sems) = rest[:-2], rest[-2:]
    for copy, _, _ in fetch(arrays, out, sems):
        copy.wait()


def joined(arrays):
    rows = sum(a.shape[0] for a in arrays)
    return pl.pallas_call(
        join_kernel,
        out_shape=jax.ShapeDtypeStruct((rows, COLS), jnp.bfloat16),
        in_specs=[ANY] * len(arrays),
        out_specs=ANY,
        scratch_shapes=[pltpu.SemaphoreType.DMA((len(arrays),))],
        compiler_params=pltpu.CompilerParams(vmem_limit_bytes=4 << 20),
        cost_estimate=pl.CostEstimate(
            flops=0, bytes_accessed=2 * rows * COLS, transcendentals=0
        ),
        name="joined",
    )(*arrays)


def halves_kernel(first, second, top, low):
    rows = top.shape[0]
    top[...] = first[:rows, :]
    low[...] = second[rows:, :]


def halves(first, second):
    rows, wide = first.shape
    half = jax.ShapeDtypeStruct((rows // 2, wide), first.dtype)
    return pl.pallas_call(
        halves_kernel,
        out_shape=(half, half),
        in_specs=[VMEM] * 2,
        out_specs=(VMEM, VMEM),
        compiler_params=pltpu.CompilerParams(vmem_limit_bytes=4 << 20),
        name="halves",
    )(first, second)


def both_ways(up, down, axis, count):
    return step(up, axis, count, 1), step(down, axis, count, -1)


def gather(half_a, half_b, flat, norm_of, tab):
    downs, ups = [half_b], [half_b]
    down, up = both_ways(half_b, half_b, "z", NZ)
    low, high = both_ways(half_a, half_a, "x", NX)
    across = step(half_a, "x", NX, 2)
    downs.append(down)
    ups.append(up)
    for _ in range(2):
        down, up = both_ways(downs[-1], ups[-1], "z", NZ)
        downs.append(down)
        ups.append(up)
    far = step(downs[-1], "z", NZ, 1)
    mine_a = joined([half_a, high, across, low])
    mine_a, down, up, tab = lax.optimization_barrier((mine_a, down, up, tab))
    mine_b = joined([half_b, *ups[1:3], up, far, down, *downs[2:0:-1]])

    down, up = both_ways(mine_a, mine_a, "z", NZ)
    low, high = both_ways(mine_b, mine_b, "x", NX)
    pieces_a = [mine_a, down, up]
    down, up, flat = lax.optimization_barrier((down, up, flat))
    down, up = both_ways(down, up, "z", NZ)
    pieces_a += [down, up]
    norm = norm_of(flat)
    down, up, norm = lax.optimization_barrier((down, up, norm))
    far_b = both_ways(*halves(low, high), "x", NX)
    down, up = both_ways(down, up, "z", NZ)
    pieces_a += [down, up]
    pieces_a += both_ways(*halves(down, up), "z", NZ)
    return pieces_a, [mine_b, low, high, *far_b], flat, norm, tab


def scores_kernel(order, k, tab, refs, weight, norm, *rest):
    arrays = rest[: len(order)]
    outs, (images, parts, whole, scaled, held, near_refs, sems) = (
        rest[len(order) : len(order) + 3],
        rest[len(order) + 3 :],
    )
    copies = fetch(arrays, whole, sems)
    [(refs_copy, _, _)] = fetch([refs], near_refs, sems, len(order))
    for copy, base, count in copies:
        copy.wait()

        def tile(i, carry, base=base):
            rows = pl.ds(pl.multiple_of(base + i * 16, 16), 16)
            scaled[rows, :] = (whole[rows, :].astype(jnp.float32) * weight[...]).astype(
                jnp.bfloat16
            )
            return carry

        lax.fori_loop(0, count // 16, tile, 0)
    images_write = pltpu.make_async_copy(whole, images, sems.at[len(order) + 4])
    images_write.start()
    refs_copy.wait()
    held[...] = (
        lax.dot_general(
            scaled[...],
            near_refs[...],
            (((1,), (1,)), ((), ())),
            preferred_element_type=jnp.float32,
        )
        - norm[...]
    )
    def compact(n, carry):
        slot = tab[k * BLOCKS + n]

        @pl.when(slot >= 0)
        def _():
            for t in range(NY):
                row = n * HALF + tab[4 * BLOCKS + 6 + k * NY + t] * 8
                to = pl.ds(pl.multiple_of(slot * 8, 8) + t * QUARTER, 8)
                parts[to, :] = held[pl.ds(pl.multiple_of(row, 8), 8), :]

        return carry

    lax.fori_loop(0, BLOCKS, compact, 0)
    done = []
    for i, (out, t, count) in enumerate(zip(outs, (2, 0, 1), (2, 1, 1))):
        source = parts.at[pl.ds(t * QUARTER, count * QUARTER), :]
        done.append(pltpu.make_async_copy(source, out, sems.at[len(order) + 1 + i]))
        done[-1].start()
    for copy in done:
        copy.wait()
    images_write.wait()


def partial_scores(order, k, tab, refs, weight, norm, pieces):
    part = jax.ShapeDtypeStruct((QUARTER, REFS), jnp.float32)
    both = jax.ShapeDtypeStruct((2 * QUARTER, REFS), jnp.float32)
    return pl.pallas_call(
        lambda *refs_: scores_kernel(order, k, *refs_),
        out_shape=(both, part, part, jax.ShapeDtypeStruct((1024, COLS), jnp.bfloat16)),
        in_specs=[SMEM, ANY, VMEM, VMEM] + [ANY] * len(pieces),
        out_specs=(ANY, ANY, ANY, ANY),
        scratch_shapes=[
            pltpu.VMEM((NY * QUARTER, REFS), jnp.float32),
            pltpu.VMEM((1024, COLS), jnp.bfloat16),
            pltpu.VMEM((1024, COLS), jnp.bfloat16),
            pltpu.VMEM((1024, REFS), jnp.float32),
            pltpu.VMEM((REFS, COLS), jnp.bfloat16),
            pltpu.SemaphoreType.DMA((len(pieces) + 5,)),
        ],
        compiler_params=pltpu.CompilerParams(vmem_limit_bytes=20 << 20),
        cost_estimate=pl.CostEstimate(
            flops=2 * 1024 * COLS * REFS, bytes_accessed=8 << 20, transcendentals=0
        ),
        name="partial_scores",
    )(tab, refs, weight, norm, *pieces)


def diagonal():
    return lax.broadcasted_iota(jnp.int32, (128, 128), 0) == lax.broadcasted_iota(
        jnp.int32, (128, 128), 1
    )


def local_kernel(kept, a0, a1, a2, b0, b1, b2, probs, stats, high, mass):
    high[...] = jnp.full(high.shape, floor_value, jnp.float32)
    mass[...] = jnp.zeros(mass.shape, jnp.float32)
    parts = []
    for first, second, third in ((a0, a1, a2), (b0, b1, b2)):
        score = first[...] + second[:QUARTER, :] + third[...]
        top = jnp.max(score, axis=1, keepdims=True)
        value = jnp.exp(score - top)
        parts.append((top, value, jnp.sum(value, axis=1, keepdims=True)))
    for j in range(MOST):
        block = kept[j]
        valid = block >= 0
        rows = slice(8 * j, 8 * j + 8)
        both = jnp.concatenate([value[rows] for _, value, _ in parts], axis=0)
        probs[16 * j : 16 * j + 16, :] = jnp.where(valid, both, 0.0).astype(jnp.bfloat16)

        @pl.when(valid)
        def _(block=block, rows=rows):
            for k, (top, _, total) in enumerate(parts):
                at = pl.ds(pl.multiple_of(block * 8, 8) + k * 256, 8)
                high[at, :] = jnp.broadcast_to(top[rows], (8, 128))
                mass[at, :] = jnp.broadcast_to(total[rows], (8, 128))

    eye = diagonal()
    for k, source in enumerate((high, mass)):
        for g in range(4):
            square = source[128 * g : 128 * g + 128, :]
            row = jnp.sum(jnp.where(eye, square, 0.0), axis=0, keepdims=True)
            stats[:, 4 * k + g : 4 * k + g + 1, :] = jnp.broadcast_to(row[None], (BLOCKS, 1, 128))


def local_stats(kept, a, b):
    return pl.pallas_call(
        local_kernel,
        out_shape=(
            jax.ShapeDtypeStruct((MOST * 16, REFS), jnp.bfloat16),
            jax.ShapeDtypeStruct((BLOCKS, 8, 128), jnp.float32),
        ),
        in_specs=[SMEM] + [VMEM] * 6,
        out_specs=(VMEM, VMEM),
        scratch_shapes=[pltpu.VMEM((512, 128), jnp.float32)] * 2,
        compiler_params=pltpu.CompilerParams(vmem_limit_bytes=16 << 20),
        name="local_stats",
    )(kept, *a, *b)


def combine_kernel(everyone, own, out):
    highs, masses = everyone[:, 0:4, :], everyone[:, 4:8, :]
    top = jnp.max(highs, axis=0)
    total = jnp.sum(masses * jnp.exp(highs - top[None]), axis=0)
    log_norm = top + jnp.log(total)
    out[0:4, :] = jnp.exp(own[0, 0:4, :] - log_norm)
    out[4:8, :] = log_norm


def combine(everyone, own):
    return pl.pallas_call(
        combine_kernel,
        out_shape=jax.ShapeDtypeStruct((8, 128), jnp.float32),
        in_specs=[VMEM, VMEM],
        out_specs=VMEM,
        name="combine_stats",
    )(everyone, own)


def fetch_both(first, second, images, sems):
    copies = fetch((first, second), images, sems)
    return [copy for copy, _, _ in copies]


def send_kernel(tab, *rest):
    scales, (own, far, near, top, low, first, second), rest = rest[:4], rest[4:11], rest[11:]
    out, rest_flipped, total, flipped, images, column, dense, probs, sems = rest
    copies = fetch_both(first, second, images, sems)
    cut = MOST * 8
    for i, source in enumerate((own, far, near)):
        probs[i] = source[...]
    probs[3, :cut, :] = top[...]
    probs[3, cut:, :] = low[...]
    eye = diagonal()
    for q, scale in enumerate(scales):
        for g in range(4):
            spread = jnp.broadcast_to(scale[g : g + 1, :], (128, 128))
            one = jnp.sum(jnp.where(eye, spread, 0.0), axis=1, keepdims=True)
            column[q, 128 * g : 128 * g + 128, :] = jnp.broadcast_to(one, (128, 128))
    for k in range(2):

        def fill(n, carry, k=k):
            slot = tab[k * BLOCKS + n]
            block = pl.ds(pl.multiple_of(tab[(2 + k) * BLOCKS + n] * 8, 8) + 256 * k, 8)
            at = pl.multiple_of(jnp.maximum(slot, 0) * 16, 16)
            parts = []
            for q in range(NY):
                owner = tab[4 * BLOCKS + 2 + q]
                value = probs[owner, pl.ds(at, 16), :].astype(jnp.float32)[8 * k : 8 * k + 8]
                factor = column[owner, block, :]
                parts.append(value * jnp.concatenate([factor] * 4, axis=1))
            rows = jnp.where(slot >= 0, jnp.concatenate(parts, axis=0), 0.0)
            dense[pl.ds(pl.multiple_of(n * HALF, HALF), HALF), :] = rows.astype(jnp.bfloat16)
            return carry

        lax.fori_loop(0, BLOCKS, fill, 0)
        flipped[:, 1024 * k : 1024 * k + 1024] = dense[...].T
    own_rows = pl.ds(pl.multiple_of(tab[4 * BLOCKS + 1], 256), 256)
    hand_on = pltpu.make_async_copy(flipped.at[own_rows, :], rest_flipped, sems.at[2])
    hand_on.start()
    for copy in copies:
        copy.wait()
    other_rows = pl.ds(pl.multiple_of(tab[4 * BLOCKS], 256), 256)
    total[...] = jnp.dot(
        flipped[other_rows, :], images[...], preferred_element_type=jnp.float32
    )
    write = pltpu.make_async_copy(total, out, sems.at[3])
    write.start()
    write.wait()
    hand_on.wait()


def keep_kernel(flipped, first, second, out, near_flipped, images, sems):
    own = pltpu.make_async_copy(flipped, near_flipped, sems.at[2])
    own.start()
    copies = fetch_both(first, second, images, sems)
    own.wait()
    for part, copy in enumerate(copies):
        copy.wait()
        span = slice(1024 * part, 1024 * part + 1024)
        value = jnp.dot(
            near_flipped[:, span], images[span, :], preferred_element_type=jnp.float32
        )
        if part == 0:
            out[...] = value
        else:
            out[...] += value


def final_kernel(mine, other, out):
    total = mine[...] + other[...]
    out[:, 0, :] = total[:, : COLS // 2]
    out[:, 1, :] = total[:, COLS // 2 :]


def weighted_sums(tab, scales, probs, images):
    half = jax.ShapeDtypeStruct((REFS // 2, COLS), jnp.float32)
    cost = pl.CostEstimate(
        flops=2 * 2048 * COLS * REFS // 2, bytes_accessed=12 << 20, transcendentals=0
    )
    out, flipped = pl.pallas_call(
        send_kernel,
        out_shape=(half, jax.ShapeDtypeStruct((REFS // 2, COLS), jnp.bfloat16)),
        in_specs=[SMEM] + [VMEM] * 9 + [ANY] * 2,
        out_specs=(ANY, ANY),
        scratch_shapes=[
            pltpu.VMEM((REFS // 2, COLS), jnp.float32),
            pltpu.VMEM((REFS, COLS), jnp.bfloat16),
            pltpu.VMEM((2048, COLS), jnp.bfloat16),
            pltpu.VMEM((NY, 512, 128), jnp.float32),
            pltpu.VMEM((1024, REFS), jnp.bfloat16),
            pltpu.VMEM((NY, MOST * 16, REFS), jnp.bfloat16),
            pltpu.SemaphoreType.DMA((4,)),
        ],
        compiler_params=pltpu.CompilerParams(vmem_limit_bytes=60 << 20),
        cost_estimate=cost,
        name="weighted_send",
    )(tab, *scales, *probs, *images)
    other = lax.ppermute(out, "dom", [(0, 1), (1, 0)])
    mine = pl.pallas_call(
        keep_kernel,
        out_shape=half,
        in_specs=[ANY] * 3,
        out_specs=VMEM,
        scratch_shapes=[
            pltpu.VMEM((REFS // 2, COLS), jnp.bfloat16),
            pltpu.VMEM((2048, COLS), jnp.bfloat16),
            pltpu.SemaphoreType.DMA((3,)),
        ],
        compiler_params=pltpu.CompilerParams(vmem_limit_bytes=60 << 20),
        cost_estimate=cost,
        name="weighted_keep",
    )(flipped, *images)
    return pl.pallas_call(
        final_kernel,
        out_shape=jax.ShapeDtypeStruct((REFS // 2, 2, COLS // 2), jnp.float32),
        in_specs=[VMEM, VMEM],
        out_specs=VMEM,
        compiler_params=pltpu.CompilerParams(vmem_limit_bytes=20 << 20),
        name="both_groups",
    )(mine, other)


def shards(references, images, noise_var, shell_of, kept_blocks):
    z, x = lax.axis_index("z"), lax.axis_index("x")
    d, y = lax.axis_index("dom"), lax.axis_index("shell")
    kept = kept_blocks.reshape(MOST)

    shells = jnp.arange(noise_var.shape[0], dtype=jnp.int32)
    picked = jnp.where(shells[:, None] == shell_of[None, :], noise_var[:, None], 0.0)
    weight = 1.0 / jnp.sum(picked, axis=0)
    weight = jnp.concatenate([weight, weight])

    def norm_of(flat):
        return 0.5 * jnp.sum(weight * jnp.square(flat.astype(jnp.float32)), axis=1)[None, :]

    near, far = y ^ 1, 3 - y
    across = 3 - near
    to_near = [(0, 1), (1, 0), (2, 3), (3, 2)]
    to_far = [(0, 3), (3, 0), (1, 2), (2, 1)]
    to_across = [(0, 2), (2, 0), (1, 3), (3, 1)]

    offsets = [b for order in (ORDER_A, ORDER_B) * 2 for piece in order for b in piece]
    offsets = jnp.array(offsets + [(0, 0)] * 14, jnp.int32)
    block = (z + offsets[:, 0]) % NZ * NX + (x + offsets[:, 1]) % NX
    index = jnp.arange(4 * BLOCKS + 14, dtype=jnp.int32)
    slots = jnp.arange(MOST, dtype=jnp.int32)
    slot = jnp.max(jnp.where(kept[None, :] == block[:, None], slots[None, :], -1), axis=1)
    rank = index - 4 * BLOCKS - 2
    tab = jnp.where(rank == y, 0, jnp.where(rank == far, 1, jnp.where(rank == near, 2, 3)))
    for at, value in enumerate((y, far, near, across, y, near, far, across)):
        tab = jnp.where(rank == NY + at, value, tab)
    tab = jnp.where(rank == -1, d * 256, jnp.where(rank == -2, (1 - d) * 256, tab))
    tab = jnp.where(index < 2 * BLOCKS, slot, jnp.where(index < 4 * BLOCKS, block, tab))

    img = images.reshape(ROWS, COLS)
    pieces_a, pieces_b, refs, norm, tab = gather(
        img[:HALF], img[HALF:], references.reshape(REFS, COLS), norm_of, tab
    )
    weight = weight[None, :]

    def summed(order, k, pieces, first, second):
        send, keep0, keep1, whole = partial_scores(order, k, tab, refs, weight, norm, pieces)
        got = lax.ppermute(send, "shell", first)
        last = lax.ppermute(keep1 + got[QUARTER:], "shell", second)
        return (keep0, got, last), whole

    sum_a, whole_a = summed(ORDER_A, 0, pieces_a, to_near, to_far)
    sum_b, whole_b = summed(ORDER_B, 1, pieces_b, to_far, to_near)

    probs, stats = local_stats(kept, sum_a, sum_b)

    from_near = lax.ppermute(probs, "shell", to_near)
    from_far = lax.ppermute(probs, "shell", to_far)
    top, low = halves(from_far, from_near)
    across_top = lax.ppermute(top, "shell", to_near)
    across_low = lax.ppermute(low, "shell", to_far)
    everyone = lax.all_to_all(
        stats, ("z", "x"), 0, 0, tiled=True
    )
    scale = combine(everyone, stats)
    scales = [scale] + [lax.ppermute(scale, "shell", to) for to in (to_far, to_near, to_across)]
    weighted = weighted_sums(
        tab,
        scales,
        (probs, from_far, from_near, across_top, across_low),
        (whole_a, whole_b),
    )

    log_norms = jnp.stack(scales)[:, 4:8, :].reshape(NY, 2, BLOCKS, 8)
    here = jnp.arange(BLOCKS, dtype=jnp.int32) == z * NX + x
    log_norms = jnp.sum(jnp.where(here[None, None, :, None], log_norms, 0.0), axis=2)
    owners = jnp.stack([y, far, near, across])[None, :] == jnp.arange(NY, dtype=jnp.int32)[:, None]
    log_norm = jnp.sum(jnp.where(owners[:, :, None, None], log_norms[None], 0.0), axis=1)
    log_norm = jnp.transpose(log_norm, (1, 0, 2)).reshape(ROWS)
    return weighted, log_norm


def solution(mesh):
    wide = Mesh(mesh.devices.reshape(NZ, NX, 2, NY), ("z", "x", "dom", "shell"))
    orient = ("z", "x")
    placed = (
        P(orient, None, "shell"),
        P(("z", "x", "dom"), None, "shell"),
        P(),
        P("shell"),
        P(orient, "dom", None),
    )
    return jax.shard_map(
        shards,
        mesh=wide,
        in_specs=placed,
        out_specs=(P(("z", "x", "dom"), None, "shell"), P(("z", "x", "dom"))),
        check_vma=False,
    )
```

```python
import jax
import jax.numpy as jnp
from jax import lax
from jax.experimental import pallas as pl
from jax.experimental.pallas import tpu as pltpu
from jax.sharding import Mesh
from jax.sharding import PartitionSpec as P

floor_value = -1e30

NZ, NX, NY = 8, 4, 4
BLOCKS = NZ * NX
ROWS = 64
HALF = 32
MOST = 24
REFS = 512
COLS = 2048
QUARTER = MOST * 8

ORDER_A = [[(dz, dx) for dx in range(4)] for dz in (0, 7, 1, 6, 2, 5, 3)] + [
    [(4, 0), (4, 1)],
    [(4, 2), (4, 3)],
]
ORDER_B = [[(dz, dx) for dz in range(8)] for dx in (0, 3, 1)] + [
    [(dz, 2) for dz in range(4)],
    [(dz, 2) for dz in range(4, 8)],
]
VMEM = pl.BlockSpec(memory_space=pltpu.VMEM)
SMEM = pl.BlockSpec(memory_space=pltpu.SMEM)
ANY = pl.BlockSpec(memory_space=pl.ANY)


def step(value, axis, count, by):
    return lax.ppermute(value, axis, [(i, (i + by) % count) for i in range(count)])


def fetch(arrays, whole, sems, first=0):
    copies, base = [], 0
    for i, piece in enumerate(arrays):
        rows = piece.shape[0]
        copy = pltpu.make_async_copy(
            piece, whole.at[pl.ds(base, rows), :], sems.at[first + i]
        )
        copy.start()
        copies.append((copy, base, rows))
        base += rows
    return copies


def join_kernel(*rest):
    arrays, (out, sems) = rest[:-2], rest[-2:]
    for copy, _, _ in fetch(arrays, out, sems):
        copy.wait()


def joined(arrays):
    rows = sum(a.shape[0] for a in arrays)
    return pl.pallas_call(
        join_kernel,
        out_shape=jax.ShapeDtypeStruct((rows, COLS), jnp.bfloat16),
        in_specs=[ANY] * len(arrays),
        out_specs=ANY,
        scratch_shapes=[pltpu.SemaphoreType.DMA((len(arrays),))],
        compiler_params=pltpu.CompilerParams(vmem_limit_bytes=4 << 20),
        cost_estimate=pl.CostEstimate(
            flops=0, bytes_accessed=2 * rows * COLS, transcendentals=0
        ),
        name="joined",
    )(*arrays)


def halves_kernel(first, second, top, low):
    rows = top.shape[0]
    top[...] = first[:rows, :]
    low[...] = second[rows:, :]


def halves(first, second):
    rows, wide = first.shape
    half = jax.ShapeDtypeStruct((rows // 2, wide), first.dtype)
    return pl.pallas_call(
        halves_kernel,
        out_shape=(half, half),
        in_specs=[VMEM] * 2,
        out_specs=(VMEM, VMEM),
        compiler_params=pltpu.CompilerParams(vmem_limit_bytes=4 << 20),
        name="halves",
    )(first, second)


def both_ways(up, down, axis, count):
    return step(up, axis, count, 1), step(down, axis, count, -1)


def gather(half_a, half_b, flat, norm_of, tab):
    downs, ups = [half_b], [half_b]
    down, up = both_ways(half_b, half_b, "z", NZ)
    low, high = both_ways(half_a, half_a, "x", NX)
    across = step(half_a, "x", NX, 2)
    downs.append(down)
    ups.append(up)
    for _ in range(2):
        down, up = both_ways(downs[-1], ups[-1], "z", NZ)
        downs.append(down)
        ups.append(up)
    far = step(downs[-1], "z", NZ, 1)
    mine_a = joined([half_a, high, across, low])
    mine_a, down, up, tab = lax.optimization_barrier((mine_a, down, up, tab))
    mine_b = joined([half_b, *ups[1:3], up, far, down, *downs[2:0:-1]])

    down, up = both_ways(mine_a, mine_a, "z", NZ)
    low, high = both_ways(mine_b, mine_b, "x", NX)
    pieces_a = [mine_a, down, up]
    down, up, flat = lax.optimization_barrier((down, up, flat))
    down, up = both_ways(down, up, "z", NZ)
    pieces_a += [down, up]
    norm = norm_of(flat)
    down, up, norm = lax.optimization_barrier((down, up, norm))
    far_b = both_ways(*halves(low, high), "x", NX)
    down, up = both_ways(down, up, "z", NZ)
    pieces_a += [down, up]
    pieces_a += both_ways(*halves(down, up), "z", NZ)
    return pieces_a, [mine_b, low, high, *far_b], flat, norm, tab


def scores_kernel(order, k, tab, refs, weight, norm, *rest):
    arrays = rest[: len(order)]
    outs, (images, parts, whole, scaled, held, near_refs, sems) = (
        rest[len(order) : len(order) + 3],
        rest[len(order) + 3 :],
    )
    copies = fetch(arrays, whole, sems)
    [(refs_copy, _, _)] = fetch([refs], near_refs, sems, len(order))
    for copy, base, count in copies:
        copy.wait()

        def tile(i, carry, base=base):
            rows = pl.ds(pl.multiple_of(base + i * 16, 16), 16)
            scaled[rows, :] = (whole[rows, :].astype(jnp.float32) * weight[...]).astype(
                jnp.bfloat16
            )
            return carry

        lax.fori_loop(0, count // 16, tile, 0)
    images_write = pltpu.make_async_copy(whole, images, sems.at[len(order) + 4])
    images_write.start()
    refs_copy.wait()
    held[...] = (
        lax.dot_general(
            scaled[...],
            near_refs[...],
            (((1,), (1,)), ((), ())),
            preferred_element_type=jnp.float32,
        )
        - norm[...]
    )
    def compact(n, carry):
        slot = tab[k * BLOCKS + n]

        @pl.when(slot >= 0)
        def _():
            for t in range(NY):
                row = n * HALF + tab[4 * BLOCKS + 6 + k * NY + t] * 8
                to = pl.ds(pl.multiple_of(slot * 8, 8) + t * QUARTER, 8)
                parts[to, :] = held[pl.ds(pl.multiple_of(row, 8), 8), :]

        return carry

    lax.fori_loop(0, BLOCKS, compact, 0)
    done = []
    for i, (out, t, count) in enumerate(zip(outs, (2, 0, 1), (2, 1, 1))):
        source = parts.at[pl.ds(t * QUARTER, count * QUARTER), :]
        done.append(pltpu.make_async_copy(source, out, sems.at[len(order) + 1 + i]))
        done[-1].start()
    for copy in done:
        copy.wait()
    images_write.wait()


def partial_scores(order, k, tab, refs, weight, norm, pieces):
    part = jax.ShapeDtypeStruct((QUARTER, REFS), jnp.float32)
    both = jax.ShapeDtypeStruct((2 * QUARTER, REFS), jnp.float32)
    return pl.pallas_call(
        lambda *refs_: scores_kernel(order, k, *refs_),
        out_shape=(both, part, part, jax.ShapeDtypeStruct((1024, COLS), jnp.bfloat16)),
        in_specs=[SMEM, ANY, VMEM, VMEM] + [ANY] * len(pieces),
        out_specs=(ANY, ANY, ANY, ANY),
        scratch_shapes=[
            pltpu.VMEM((NY * QUARTER, REFS), jnp.float32),
            pltpu.VMEM((1024, COLS), jnp.bfloat16),
            pltpu.VMEM((1024, COLS), jnp.bfloat16),
            pltpu.VMEM((1024, REFS), jnp.float32),
            pltpu.VMEM((REFS, COLS), jnp.bfloat16),
            pltpu.SemaphoreType.DMA((len(pieces) + 5,)),
        ],
        compiler_params=pltpu.CompilerParams(vmem_limit_bytes=44 << 20),
        cost_estimate=pl.CostEstimate(
            flops=2 * 1024 * COLS * REFS, bytes_accessed=8 << 20, transcendentals=0
        ),
        name="partial_scores",
    )(tab, refs, weight, norm, *pieces)


def diagonal():
    return lax.broadcasted_iota(jnp.int32, (128, 128), 0) == lax.broadcasted_iota(
        jnp.int32, (128, 128), 1
    )


def local_kernel(kept, a0, a1, a2, b0, b1, b2, probs, stats, high, mass):
    high[...] = jnp.full(high.shape, floor_value, jnp.float32)
    mass[...] = jnp.zeros(mass.shape, jnp.float32)
    parts = []
    for first, second, third in ((a0, a1, a2), (b0, b1, b2)):
        score = first[...] + second[:QUARTER, :] + third[...]
        top = jnp.max(score, axis=1, keepdims=True)
        value = jnp.exp(score - top)
        parts.append((top, value, jnp.sum(value, axis=1, keepdims=True)))
    for j in range(MOST):
        block = kept[j]
        valid = block >= 0
        rows = slice(8 * j, 8 * j + 8)
        both = jnp.concatenate([value[rows] for _, value, _ in parts], axis=0)
        probs[16 * j : 16 * j + 16, :] = jnp.where(valid, both, 0.0).astype(jnp.bfloat16)

        @pl.when(valid)
        def _(block=block, rows=rows):
            for k, (top, _, total) in enumerate(parts):
                at = pl.ds(pl.multiple_of(block * 8, 8) + k * 256, 8)
                high[at, :] = jnp.broadcast_to(top[rows], (8, 128))
                mass[at, :] = jnp.broadcast_to(total[rows], (8, 128))

    eye = diagonal()
    for k, source in enumerate((high, mass)):
        for g in range(4):
            square = source[128 * g : 128 * g + 128, :]
            row = jnp.sum(jnp.where(eye, square, 0.0), axis=0, keepdims=True)
            stats[:, 4 * k + g : 4 * k + g + 1, :] = jnp.broadcast_to(row[None], (BLOCKS, 1, 128))


def local_stats(kept, a, b):
    return pl.pallas_call(
        local_kernel,
        out_shape=(
            jax.ShapeDtypeStruct((MOST * 16, REFS), jnp.bfloat16),
            jax.ShapeDtypeStruct((BLOCKS, 8, 128), jnp.float32),
        ),
        in_specs=[SMEM] + [VMEM] * 6,
        out_specs=(VMEM, VMEM),
        scratch_shapes=[pltpu.VMEM((512, 128), jnp.float32)] * 2,
        compiler_params=pltpu.CompilerParams(vmem_limit_bytes=16 << 20),
        name="local_stats",
    )(kept, *a, *b)


def combine_kernel(everyone, own, out):
    highs, masses = everyone[:, 0:4, :], everyone[:, 4:8, :]
    top = jnp.max(highs, axis=0)
    total = jnp.sum(masses * jnp.exp(highs - top[None]), axis=0)
    log_norm = top + jnp.log(total)
    out[0:4, :] = jnp.exp(own[0, 0:4, :] - log_norm)
    out[4:8, :] = log_norm


def combine(everyone, own):
    return pl.pallas_call(
        combine_kernel,
        out_shape=jax.ShapeDtypeStruct((8, 128), jnp.float32),
        in_specs=[VMEM, VMEM],
        out_specs=VMEM,
        compiler_params=pltpu.CompilerParams(vmem_limit_bytes=4 << 20),
        name="combine_stats",
    )(everyone, own)


def lay_kernel(tab, own, far, near, top, low, first, second, flipped, images, dense, probs, sems):
    copies = [copy for copy, _, _ in fetch((first, second), images, sems)]
    cut = MOST * 8
    for i, source in enumerate((own, far, near)):
        probs[i] = source[...]
    probs[3, :cut, :] = top[...]
    probs[3, cut:, :] = low[...]
    for k in range(2):

        def fill(n, carry, k=k):
            slot = tab[k * BLOCKS + n]
            at = pl.ds(pl.multiple_of(jnp.maximum(slot, 0) * 16, 16), 16)
            parts = []
            for q in range(NY):
                owner = tab[4 * BLOCKS + 2 + q]
                parts.append(probs[owner, at, :].astype(jnp.float32)[8 * k : 8 * k + 8])
            rows = jnp.where(slot >= 0, jnp.concatenate(parts, axis=0), 0.0)
            dense[pl.ds(pl.multiple_of(n * HALF, HALF), HALF), :] = rows.astype(jnp.bfloat16)
            return carry

        lax.fori_loop(0, BLOCKS, fill, 0)
        flipped[:, 1024 * k : 1024 * k + 1024] = dense[...].T
    for copy in copies:
        copy.wait()


def scaled_rows(flipped, factor, base, out):
    def tile(i, carry):
        at = pl.multiple_of(i * 16, 16)
        rows = flipped[pl.ds(pl.multiple_of(base + at, 16), 16), :].astype(jnp.float32)
        out[pl.ds(at, 16), :] = (rows * factor[...]).astype(jnp.bfloat16)
        return carry

    lax.fori_loop(0, REFS // 32, tile, 0)


def send_kernel(tab, *rest):
    scales, (flipped, images, out, factor, total, half, column, ordered, sem) = rest[:4], rest[4:]
    eye = diagonal()
    for q, scale in enumerate(scales):
        for g in range(4):
            spread = jnp.broadcast_to(scale[g : g + 1, :], (128, 128))
            one = jnp.sum(jnp.where(eye, spread, 0.0), axis=1, keepdims=True)
            column[q, 128 * g : 128 * g + 128, :] = jnp.broadcast_to(one, (128, 128))
    for k in range(2):

        def fill(n, carry, k=k):
            block = pl.multiple_of(tab[(2 + k) * BLOCKS + n] * 8, 8) + 256 * k
            for q in range(NY):
                to = pl.multiple_of(n * HALF, HALF) + 1024 * k + 8 * q
                ordered[pl.ds(to, 8), :] = column[
                    tab[4 * BLOCKS + 2 + q], pl.ds(block, 8), :
                ]
            return carry

        lax.fori_loop(0, BLOCKS, fill, 0)
    for g in range(16):
        square = ordered[128 * g : 128 * g + 128, :]
        factor[:, 128 * g : 128 * g + 128] = jnp.sum(
            jnp.where(eye, square, 0.0), axis=0, keepdims=True
        )
    scaled_rows(flipped, factor, tab[4 * BLOCKS], half)
    total[...] = jnp.dot(half[...], images[...], preferred_element_type=jnp.float32)
    write = pltpu.make_async_copy(total, out, sem)
    write.start()
    write.wait()


def keep_kernel(tab, *rest):
    scales, (flipped, images, factor, out, norms, half) = rest[:4], rest[4:]
    scaled_rows(flipped, factor, tab[4 * BLOCKS + 1], half)
    out[...] = jnp.dot(half[...], images[...], preferred_element_type=jnp.float32)
    home = tab[4 * BLOCKS + 14]
    lane = lax.broadcasted_iota(jnp.int32, (1, 128), 1)
    spot = home % 16
    total = jnp.zeros((1, 128), jnp.float32)
    for k in range(2):
        for i, scale in enumerate(scales):
            first, second = scale[4 + 2 * k : 5 + 2 * k, :], scale[5 + 2 * k : 6 + 2 * k, :]
            row = jnp.where(home >= 16, second, first)
            row = jnp.where(lane // 8 == spot, row, 0.0)
            q = tab[4 * BLOCKS + 6 + i]
            total += pltpu.roll(row, (HALF * k + q * 8 + 128 - spot * 8) % 128, 1)
    norms[...] = total[:, :ROWS]


def final_kernel(mine, other, out, near, sems):
    copies = []
    for i in range(4):
        rows = pl.ds(64 * i, 64)
        copies.append(pltpu.make_async_copy(other.at[rows, :], near.at[rows, :], sems.at[i]))
        copies[-1].start()
    for i, copy in enumerate(copies):
        copy.wait()
        rows = slice(64 * i, 64 * i + 64)
        total = mine[rows, :] + near[rows, :]
        out[rows, 0, :] = total[:, : COLS // 2]
        out[rows, 1, :] = total[:, COLS // 2 :]


def weighted_sums(tab, scales, probs, pieces):
    half = jax.ShapeDtypeStruct((REFS // 2, COLS), jnp.float32)
    cost = pl.CostEstimate(
        flops=2 * 2048 * COLS * REFS // 2, bytes_accessed=12 << 20, transcendentals=0
    )
    flipped, images = pl.pallas_call(
        lay_kernel,
        out_shape=(
            jax.ShapeDtypeStruct((REFS, COLS), jnp.bfloat16),
            jax.ShapeDtypeStruct((2048, COLS), jnp.bfloat16),
        ),
        in_specs=[SMEM] + [VMEM] * 5 + [ANY] * 2,
        out_specs=(VMEM, VMEM),
        scratch_shapes=[
            pltpu.VMEM((1024, REFS), jnp.bfloat16),
            pltpu.VMEM((NY, MOST * 16, REFS), jnp.bfloat16),
            pltpu.SemaphoreType.DMA((2,)),
        ],
        compiler_params=pltpu.CompilerParams(vmem_limit_bytes=16 << 20),
        name="lay_posteriors",
    )(tab, *probs, *pieces)
    out, factor = pl.pallas_call(
        send_kernel,
        out_shape=(half, jax.ShapeDtypeStruct((1, COLS), jnp.float32)),
        in_specs=[SMEM] + [VMEM] * 6,
        out_specs=(ANY, VMEM),
        scratch_shapes=[
            pltpu.VMEM((REFS // 2, COLS), jnp.float32),
            pltpu.VMEM((REFS // 2, COLS), jnp.bfloat16),
            pltpu.VMEM((NY, 512, 128), jnp.float32),
            pltpu.VMEM((2048, 128), jnp.float32),
            pltpu.SemaphoreType.DMA,
        ],
        compiler_params=pltpu.CompilerParams(vmem_limit_bytes=16 << 20),
        cost_estimate=cost,
        name="weighted_send",
    )(tab, *scales, flipped, images)
    other = lax.ppermute(out, "dom", [(0, 1), (1, 0)])
    mine, norms = pl.pallas_call(
        keep_kernel,
        out_shape=(half, jax.ShapeDtypeStruct((1, ROWS), jnp.float32)),
        in_specs=[SMEM] + [VMEM] * 7,
        out_specs=(VMEM, VMEM),
        scratch_shapes=[pltpu.VMEM((REFS // 2, COLS), jnp.bfloat16)],
        compiler_params=pltpu.CompilerParams(vmem_limit_bytes=16 << 20),
        cost_estimate=cost,
        name="weighted_keep",
    )(tab, *scales, flipped, images, factor)
    weighted = pl.pallas_call(
        final_kernel,
        out_shape=jax.ShapeDtypeStruct((REFS // 2, 2, COLS // 2), jnp.float32),
        in_specs=[VMEM, ANY],
        out_specs=VMEM,
        scratch_shapes=[
            pltpu.VMEM((REFS // 2, COLS), jnp.float32),
            pltpu.SemaphoreType.DMA((4,)),
        ],
        compiler_params=pltpu.CompilerParams(vmem_limit_bytes=16 << 20),
        name="both_groups",
    )(mine, other)
    return weighted, norms.reshape(ROWS)


def shards(references, images, noise_var, shell_of, kept_blocks):
    z, x = lax.axis_index("z"), lax.axis_index("x")
    d, y = lax.axis_index("dom"), lax.axis_index("shell")
    kept = kept_blocks.reshape(MOST)

    shells = jnp.arange(noise_var.shape[0], dtype=jnp.int32)
    picked = jnp.where(shells[:, None] == shell_of[None, :], noise_var[:, None], 0.0)
    weight = 1.0 / jnp.sum(picked, axis=0)
    weight = jnp.concatenate([weight, weight])

    def norm_of(flat):
        return 0.5 * jnp.sum(weight * jnp.square(flat.astype(jnp.float32)), axis=1)[None, :]

    near, far = y ^ 1, 3 - y
    across = 3 - near
    to_near = [(0, 1), (1, 0), (2, 3), (3, 2)]
    to_far = [(0, 3), (3, 0), (1, 2), (2, 1)]
    to_across = [(0, 2), (2, 0), (1, 3), (3, 1)]

    offsets = [b for order in (ORDER_A, ORDER_B) * 2 for piece in order for b in piece]
    offsets = jnp.array(offsets + [(0, 0)] * 15, jnp.int32)
    block = (z + offsets[:, 0]) % NZ * NX + (x + offsets[:, 1]) % NX
    index = jnp.arange(4 * BLOCKS + 15, dtype=jnp.int32)
    slots = jnp.arange(MOST, dtype=jnp.int32)
    slot = jnp.max(jnp.where(kept[None, :] == block[:, None], slots[None, :], -1), axis=1)
    rank = index - 4 * BLOCKS - 2
    tab = jnp.where(rank == y, 0, jnp.where(rank == far, 1, jnp.where(rank == near, 2, 3)))
    for at, value in enumerate(
        (y, far, near, across, y, near, far, across, z * NX + x)
    ):
        tab = jnp.where(rank == NY + at, value, tab)
    tab = jnp.where(rank == -1, d * 256, jnp.where(rank == -2, (1 - d) * 256, tab))
    tab = jnp.where(index < 2 * BLOCKS, slot, jnp.where(index < 4 * BLOCKS, block, tab))

    img = images.reshape(ROWS, COLS)
    pieces_a, pieces_b, refs, norm, tab = gather(
        img[:HALF], img[HALF:], references.reshape(REFS, COLS), norm_of, tab
    )
    weight = weight[None, :]

    def summed(order, k, pieces, first, second):
        send, keep0, keep1, whole = partial_scores(order, k, tab, refs, weight, norm, pieces)
        got = lax.ppermute(send, "shell", first)
        last = lax.ppermute(keep1 + got[QUARTER:], "shell", second)
        return (keep0, got, last), whole

    sum_a, whole_a = summed(ORDER_A, 0, pieces_a, to_near, to_far)
    sum_b, whole_b = summed(ORDER_B, 1, pieces_b, to_far, to_near)

    probs, stats = local_stats(kept, sum_a, sum_b)

    from_near = lax.ppermute(probs, "shell", to_near)
    from_far = lax.ppermute(probs, "shell", to_far)
    top, low = halves(from_far, from_near)
    across_top = lax.ppermute(top, "shell", to_near)
    across_low = lax.ppermute(low, "shell", to_far)
    everyone = lax.all_to_all(
        stats, ("z", "x"), 0, 0, tiled=True
    )
    scale = combine(everyone, stats)
    scales = [scale] + [lax.ppermute(scale, "shell", to) for to in (to_far, to_near, to_across)]
    return weighted_sums(
        tab,
        scales,
        (probs, from_far, from_near, across_top, across_low),
        (whole_a, whole_b),
    )


def solution(mesh):
    wide = Mesh(mesh.devices.reshape(NZ, NX, 2, NY), ("z", "x", "dom", "shell"))
    orient = ("z", "x")
    placed = (
        P(orient, None, "shell"),
        P(("z", "x", "dom"), None, "shell"),
        P(),
        P("shell"),
        P(orient, "dom", None),
    )
    return jax.shard_map(
        shards,
        mesh=wide,
        in_specs=placed,
        out_specs=(P(("z", "x", "dom"), None, "shell"), P(("z", "x", "dom"))),
        check_vma=False,
    )
```

```python
import jax
import jax.numpy as jnp
from jax import lax
from jax.experimental import pallas as pl
from jax.experimental.pallas import tpu as pltpu
from jax.sharding import Mesh
from jax.sharding import PartitionSpec as P

floor_value = -1e30

NZ, NX, NY = 8, 4, 4
BLOCKS = NZ * NX
ROWS = 64
HALF = 32
MOST = 24
REFS = 512
COLS = 2048
QUARTER = MOST * 8

ORDER_A = [[(dz, dx) for dx in range(4)] for dz in (0, 7, 1, 6, 2, 5, 3)] + [
    [(4, 0), (4, 1)],
    [(4, 2), (4, 3)],
]
ORDER_B = [[(dz, dx) for dz in range(8)] for dx in (0, 3, 1)] + [
    [(dz, 2) for dz in range(4)],
    [(dz, 2) for dz in range(4, 8)],
]
VMEM = pl.BlockSpec(memory_space=pltpu.VMEM)
SMEM = pl.BlockSpec(memory_space=pltpu.SMEM)
ANY = pl.BlockSpec(memory_space=pl.ANY)


def step(value, axis, count, by):
    return lax.ppermute(value, axis, [(i, (i + by) % count) for i in range(count)])


def fetch(arrays, whole, sems, first=0):
    copies, base = [], 0
    for i, piece in enumerate(arrays):
        rows = piece.shape[0]
        copy = pltpu.make_async_copy(
            piece, whole.at[pl.ds(base, rows), :], sems.at[first + i]
        )
        copy.start()
        copies.append((copy, base, rows))
        base += rows
    return copies


def join_kernel(*rest):
    arrays, (out, sems) = rest[:-2], rest[-2:]
    for copy, _, _ in fetch(arrays, out, sems):
        copy.wait()


def joined(arrays):
    rows = sum(a.shape[0] for a in arrays)
    return pl.pallas_call(
        join_kernel,
        out_shape=jax.ShapeDtypeStruct((rows, COLS), jnp.bfloat16),
        in_specs=[ANY] * len(arrays),
        out_specs=ANY,
        scratch_shapes=[pltpu.SemaphoreType.DMA((len(arrays),))],
        compiler_params=pltpu.CompilerParams(vmem_limit_bytes=4 << 20),
        cost_estimate=pl.CostEstimate(
            flops=0, bytes_accessed=2 * rows * COLS, transcendentals=0
        ),
        name="joined",
    )(*arrays)


def halves_kernel(first, second, top, low):
    rows = top.shape[0]
    top[...] = first[:rows, :]
    low[...] = second[rows:, :]


def halves(first, second):
    rows, wide = first.shape
    half = jax.ShapeDtypeStruct((rows // 2, wide), first.dtype)
    return pl.pallas_call(
        halves_kernel,
        out_shape=(half, half),
        in_specs=[VMEM] * 2,
        out_specs=(VMEM, VMEM),
        compiler_params=pltpu.CompilerParams(vmem_limit_bytes=4 << 20),
        name="halves",
    )(first, second)


def both_ways(up, down, axis, count):
    return step(up, axis, count, 1), step(down, axis, count, -1)


def gather(half_a, half_b, flat, norm_of, weight, tab):
    downs, ups = [half_b], [half_b]
    down, up = both_ways(half_b, half_b, "z", NZ)
    low, high = both_ways(half_a, half_a, "x", NX)
    across = step(half_a, "x", NX, 2)
    downs.append(down)
    ups.append(up)
    for _ in range(2):
        down, up = both_ways(downs[-1], ups[-1], "z", NZ)
        downs.append(down)
        ups.append(up)
    far = step(downs[-1], "z", NZ, 1)
    mine_a = joined([half_a, high, across, low])
    mine_a, down, up, tab = lax.optimization_barrier((mine_a, down, up, tab))
    mine_b = joined([half_b, *ups[1:3], up, far, down, *downs[2:0:-1]])

    down, up = both_ways(mine_a, mine_a, "z", NZ)
    low, high = both_ways(mine_b, mine_b, "x", NX)
    pieces_a = [mine_a, down, up]
    down, up, flat = lax.optimization_barrier((down, up, flat))
    down, up = both_ways(down, up, "z", NZ)
    pieces_a += [down, up]
    norm = norm_of(flat)
    down, up, norm = lax.optimization_barrier((down, up, norm))
    far_b = both_ways(*halves(low, high), "x", NX)
    down, up = both_ways(down, up, "z", NZ)
    early, images = early_scores(flat, weight, norm, pieces_a)
    early, down, up = lax.optimization_barrier((early, down, up))
    pieces_a = [down, up, *both_ways(*halves(down, up), "z", NZ)]
    return early, images, pieces_a, [mine_b, low, high, *far_b], flat, norm, tab


def scaled_product(arrays, refs, weight, norm, whole, scaled, near_refs, images, sems):
    copies = fetch(arrays, whole, sems)
    [(refs_copy, _, _)] = fetch([refs], near_refs, sems, len(arrays))
    for copy, base, count in copies:
        copy.wait()

        def tile(i, carry, base=base):
            rows = pl.ds(pl.multiple_of(base + i * 16, 16), 16)
            scaled[rows, :] = (whole[rows, :].astype(jnp.float32) * weight[...]).astype(
                jnp.bfloat16
            )
            return carry

        lax.fori_loop(0, count // 16, tile, 0)
    images_write = pltpu.make_async_copy(whole, images, sems.at[len(arrays) + 1])
    images_write.start()
    refs_copy.wait()
    value = lax.dot_general(
        scaled[...],
        near_refs[...],
        (((1,), (1,)), ((), ())),
        preferred_element_type=jnp.float32,
    )
    return value - norm[...], images_write


def early_kernel(refs, weight, norm, *rest):
    arrays, (out, images, held, whole, scaled, near_refs, sems) = rest[:-7], rest[-7:]
    held[...], images_write = scaled_product(
        arrays, refs, weight, norm, whole, scaled, near_refs, images, sems
    )
    write = pltpu.make_async_copy(held, out, sems.at[len(arrays) + 2])
    write.start()
    write.wait()
    images_write.wait()


def early_scores(refs, weight, norm, pieces):
    rows = sum(p.shape[0] for p in pieces)
    return pl.pallas_call(
        early_kernel,
        out_shape=(
            jax.ShapeDtypeStruct((rows, REFS), jnp.float32),
            jax.ShapeDtypeStruct((rows, COLS), jnp.bfloat16),
        ),
        in_specs=[ANY, VMEM, VMEM] + [ANY] * len(pieces),
        out_specs=(ANY, ANY),
        scratch_shapes=[
            pltpu.VMEM((rows, REFS), jnp.float32),
            pltpu.VMEM((rows, COLS), jnp.bfloat16),
            pltpu.VMEM((rows, COLS), jnp.bfloat16),
            pltpu.VMEM((REFS, COLS), jnp.bfloat16),
            pltpu.SemaphoreType.DMA((len(pieces) + 3,)),
        ],
        compiler_params=pltpu.CompilerParams(vmem_limit_bytes=44 << 20),
        cost_estimate=pl.CostEstimate(
            flops=2 * rows * COLS * REFS, bytes_accessed=8 << 20, transcendentals=0
        ),
        name="early_scores",
    )(refs, weight, norm, *pieces)


def scores_kernel(k, pieces, first, tab, refs, weight, norm, *rest):
    early, arrays, rest = rest[: first > 0], rest[first > 0 :][:pieces], rest[first > 0 :][pieces:]
    outs, (images, parts, whole, scaled, held, near_refs, sems) = rest[:3], rest[3:]
    if early:
        early_copy = pltpu.make_async_copy(
            early[0], held.at[pl.ds(0, first), :], sems.at[pieces + 2]
        )
        early_copy.start()
    held[first:, :], images_write = scaled_product(
        arrays, refs, weight, norm, whole, scaled, near_refs, images, sems
    )
    if early:
        early_copy.wait()

    def compact(n, carry):
        slot = tab[k * BLOCKS + n]

        @pl.when(slot >= 0)
        def _():
            for t in range(NY):
                row = n * HALF + tab[4 * BLOCKS + 6 + k * NY + t] * 8
                to = pl.ds(pl.multiple_of(slot * 8, 8) + t * QUARTER, 8)
                parts[to, :] = held[pl.ds(pl.multiple_of(row, 8), 8), :]

        return carry

    lax.fori_loop(0, BLOCKS, compact, 0)
    done = []
    for i, (out, t, count) in enumerate(zip(outs, (2, 0, 1), (2, 1, 1))):
        source = parts.at[pl.ds(t * QUARTER, count * QUARTER), :]
        done.append(pltpu.make_async_copy(source, out, sems.at[pieces + 3 + i]))
        done[-1].start()
    for copy in done:
        copy.wait()
    images_write.wait()


def partial_scores(k, tab, refs, weight, norm, pieces, early=()):
    part = jax.ShapeDtypeStruct((QUARTER, REFS), jnp.float32)
    both = jax.ShapeDtypeStruct((2 * QUARTER, REFS), jnp.float32)
    rows = sum(p.shape[0] for p in pieces)
    return pl.pallas_call(
        lambda *refs_: scores_kernel(k, len(pieces), 1024 - rows, *refs_),
        out_shape=(both, part, part, jax.ShapeDtypeStruct((rows, COLS), jnp.bfloat16)),
        in_specs=[SMEM, ANY, VMEM, VMEM] + [ANY] * (len(early) + len(pieces)),
        out_specs=(ANY, ANY, ANY, ANY),
        scratch_shapes=[
            pltpu.VMEM((NY * QUARTER, REFS), jnp.float32),
            pltpu.VMEM((rows, COLS), jnp.bfloat16),
            pltpu.VMEM((rows, COLS), jnp.bfloat16),
            pltpu.VMEM((1024, REFS), jnp.float32),
            pltpu.VMEM((REFS, COLS), jnp.bfloat16),
            pltpu.SemaphoreType.DMA((len(pieces) + 6,)),
        ],
        compiler_params=pltpu.CompilerParams(vmem_limit_bytes=44 << 20),
        cost_estimate=pl.CostEstimate(
            flops=2 * rows * COLS * REFS, bytes_accessed=8 << 20, transcendentals=0
        ),
        name="partial_scores",
    )(tab, refs, weight, norm, *early, *pieces)


def diagonal():
    return lax.broadcasted_iota(jnp.int32, (128, 128), 0) == lax.broadcasted_iota(
        jnp.int32, (128, 128), 1
    )


def local_kernel(kept, a0, a1, a2, b0, b1, b2, probs, stats, high, mass):
    high[...] = jnp.full(high.shape, floor_value, jnp.float32)
    mass[...] = jnp.zeros(mass.shape, jnp.float32)
    parts = []
    for first, second, third in ((a0, a1, a2), (b0, b1, b2)):
        score = first[...] + second[:QUARTER, :] + third[...]
        top = jnp.max(score, axis=1, keepdims=True)
        value = jnp.exp(score - top)
        parts.append((top, value, jnp.sum(value, axis=1, keepdims=True)))
    for j in range(MOST):
        block = kept[j]
        valid = block >= 0
        rows = slice(8 * j, 8 * j + 8)
        both = jnp.concatenate([value[rows] for _, value, _ in parts], axis=0)
        probs[16 * j : 16 * j + 16, :] = jnp.where(valid, both, 0.0).astype(jnp.bfloat16)

        @pl.when(valid)
        def _(block=block, rows=rows):
            for k, (top, _, total) in enumerate(parts):
                at = pl.ds(pl.multiple_of(block * 8, 8) + k * 256, 8)
                high[at, :] = jnp.broadcast_to(top[rows], (8, 128))
                mass[at, :] = jnp.broadcast_to(total[rows], (8, 128))

    eye = diagonal()
    for k, source in enumerate((high, mass)):
        for g in range(4):
            square = source[128 * g : 128 * g + 128, :]
            row = jnp.sum(jnp.where(eye, square, 0.0), axis=0, keepdims=True)
            stats[:, 4 * k + g : 4 * k + g + 1, :] = jnp.broadcast_to(row[None], (BLOCKS, 1, 128))


def local_stats(kept, a, b):
    return pl.pallas_call(
        local_kernel,
        out_shape=(
            jax.ShapeDtypeStruct((MOST * 16, REFS), jnp.bfloat16),
            jax.ShapeDtypeStruct((BLOCKS, 8, 128), jnp.float32),
        ),
        in_specs=[SMEM] + [VMEM] * 6,
        out_specs=(VMEM, VMEM),
        scratch_shapes=[pltpu.VMEM((512, 128), jnp.float32)] * 2,
        compiler_params=pltpu.CompilerParams(vmem_limit_bytes=16 << 20),
        name="local_stats",
    )(kept, *a, *b)


def combine_kernel(everyone, own, out):
    highs, masses = everyone[:, 0:4, :], everyone[:, 4:8, :]
    top = jnp.max(highs, axis=0)
    total = jnp.sum(masses * jnp.exp(highs - top[None]), axis=0)
    log_norm = top + jnp.log(total)
    out[0:4, :] = jnp.exp(own[0, 0:4, :] - log_norm)
    out[4:8, :] = log_norm


def combine(everyone, own):
    return pl.pallas_call(
        combine_kernel,
        out_shape=jax.ShapeDtypeStruct((8, 128), jnp.float32),
        in_specs=[VMEM, VMEM],
        out_specs=VMEM,
        compiler_params=pltpu.CompilerParams(vmem_limit_bytes=4 << 20),
        name="combine_stats",
    )(everyone, own)


def lay_kernel(tab, own, far, near, top, low, flipped, dense, probs):
    cut = MOST * 8
    for i, source in enumerate((own, far, near)):
        probs[i] = source[...]
    probs[3, :cut, :] = top[...]
    probs[3, cut:, :] = low[...]
    for k in range(2):

        def fill(n, carry, k=k):
            slot = tab[k * BLOCKS + n]
            at = pl.ds(pl.multiple_of(jnp.maximum(slot, 0) * 16, 16), 16)
            parts = []
            for q in range(NY):
                owner = tab[4 * BLOCKS + 2 + q]
                parts.append(probs[owner, at, :].astype(jnp.float32)[8 * k : 8 * k + 8])
            rows = jnp.where(slot >= 0, jnp.concatenate(parts, axis=0), 0.0)
            dense[pl.ds(pl.multiple_of(n * HALF, HALF), HALF), :] = rows.astype(jnp.bfloat16)
            return carry

        lax.fori_loop(0, BLOCKS, fill, 0)
        flipped[:, 1024 * k : 1024 * k + 1024] = dense[...].T


def product(half, images):
    total, at = None, 0
    for piece in images:
        rows = piece.shape[0]
        value = jnp.dot(
            half[:, at : at + rows], piece[...], preferred_element_type=jnp.float32
        )
        total = value if total is None else total + value
        at += rows
    return total


def scaled_rows(flipped, factor, base, out):
    def tile(i, carry):
        at = pl.multiple_of(i * 16, 16)
        rows = flipped[pl.ds(pl.multiple_of(base + at, 16), 16), :].astype(jnp.float32)
        out[pl.ds(at, 16), :] = (rows * factor[...]).astype(jnp.bfloat16)
        return carry

    lax.fori_loop(0, REFS // 32, tile, 0)


def send_kernel(tab, *rest):
    scales, flipped, images, rest = rest[:4], rest[4], rest[5:8], rest[8:]
    out, factor, total, half, column, ordered, sem = rest
    eye = diagonal()
    for q, scale in enumerate(scales):
        for g in range(4):
            spread = jnp.broadcast_to(scale[g : g + 1, :], (128, 128))
            one = jnp.sum(jnp.where(eye, spread, 0.0), axis=1, keepdims=True)
            column[q, 128 * g : 128 * g + 128, :] = jnp.broadcast_to(one, (128, 128))
    for k in range(2):

        def fill(n, carry, k=k):
            block = pl.multiple_of(tab[(2 + k) * BLOCKS + n] * 8, 8) + 256 * k
            for q in range(NY):
                to = pl.multiple_of(n * HALF, HALF) + 1024 * k + 8 * q
                ordered[pl.ds(to, 8), :] = column[
                    tab[4 * BLOCKS + 2 + q], pl.ds(block, 8), :
                ]
            return carry

        lax.fori_loop(0, BLOCKS, fill, 0)
    for g in range(16):
        square = ordered[128 * g : 128 * g + 128, :]
        factor[:, 128 * g : 128 * g + 128] = jnp.sum(
            jnp.where(eye, square, 0.0), axis=0, keepdims=True
        )
    scaled_rows(flipped, factor, tab[4 * BLOCKS], half)
    total[...] = product(half, images)
    write = pltpu.make_async_copy(total, out, sem)
    write.start()
    write.wait()


def keep_kernel(tab, *rest):
    scales, flipped, images, rest = rest[:4], rest[4], rest[5:8], rest[8:]
    factor, out, norms, half = rest
    scaled_rows(flipped, factor, tab[4 * BLOCKS + 1], half)
    out[...] = product(half, images)
    home = tab[4 * BLOCKS + 14]
    lane = lax.broadcasted_iota(jnp.int32, (1, 128), 1)
    spot = home % 16
    total = jnp.zeros((1, 128), jnp.float32)
    for k in range(2):
        for i, scale in enumerate(scales):
            first, second = scale[4 + 2 * k : 5 + 2 * k, :], scale[5 + 2 * k : 6 + 2 * k, :]
            row = jnp.where(home >= 16, second, first)
            row = jnp.where(lane // 8 == spot, row, 0.0)
            q = tab[4 * BLOCKS + 6 + i]
            total += pltpu.roll(row, (HALF * k + q * 8 + 128 - spot * 8) % 128, 1)
    norms[...] = total[:, :ROWS]


def final_kernel(mine, other, out, near, sems):
    copies = []
    for i in range(4):
        rows = pl.ds(64 * i, 64)
        copies.append(pltpu.make_async_copy(other.at[rows, :], near.at[rows, :], sems.at[i]))
        copies[-1].start()
    for i, copy in enumerate(copies):
        copy.wait()
        rows = slice(64 * i, 64 * i + 64)
        total = mine[rows, :] + near[rows, :]
        out[rows, 0, :] = total[:, : COLS // 2]
        out[rows, 1, :] = total[:, COLS // 2 :]


def weighted_sums(tab, scales, probs, images):
    half = jax.ShapeDtypeStruct((REFS // 2, COLS), jnp.float32)
    cost = pl.CostEstimate(
        flops=2 * 2048 * COLS * REFS // 2, bytes_accessed=12 << 20, transcendentals=0
    )
    flipped = pl.pallas_call(
        lay_kernel,
        out_shape=jax.ShapeDtypeStruct((REFS, COLS), jnp.bfloat16),
        in_specs=[SMEM] + [VMEM] * 5,
        out_specs=VMEM,
        scratch_shapes=[
            pltpu.VMEM((1024, REFS), jnp.bfloat16),
            pltpu.VMEM((NY, MOST * 16, REFS), jnp.bfloat16),
        ],
        compiler_params=pltpu.CompilerParams(vmem_limit_bytes=16 << 20),
        cost_estimate=pl.CostEstimate(
            flops=0, bytes_accessed=16 << 20, transcendentals=0
        ),
        name="lay_posteriors",
    )(tab, *probs)
    out, factor = pl.pallas_call(
        send_kernel,
        out_shape=(half, jax.ShapeDtypeStruct((1, COLS), jnp.float32)),
        in_specs=[SMEM] + [VMEM] * 8,
        out_specs=(ANY, VMEM),
        scratch_shapes=[
            pltpu.VMEM((REFS // 2, COLS), jnp.float32),
            pltpu.VMEM((REFS // 2, COLS), jnp.bfloat16),
            pltpu.VMEM((NY, 512, 128), jnp.float32),
            pltpu.VMEM((2048, 128), jnp.float32),
            pltpu.SemaphoreType.DMA,
        ],
        compiler_params=pltpu.CompilerParams(vmem_limit_bytes=16 << 20),
        cost_estimate=cost,
        name="weighted_send",
    )(tab, *scales, flipped, *images)
    other = lax.ppermute(out, "dom", [(0, 1), (1, 0)])
    mine, norms = pl.pallas_call(
        keep_kernel,
        out_shape=(half, jax.ShapeDtypeStruct((1, ROWS), jnp.float32)),
        in_specs=[SMEM] + [VMEM] * 9,
        out_specs=(VMEM, VMEM),
        scratch_shapes=[pltpu.VMEM((REFS // 2, COLS), jnp.bfloat16)],
        compiler_params=pltpu.CompilerParams(vmem_limit_bytes=16 << 20),
        cost_estimate=cost,
        name="weighted_keep",
    )(tab, *scales, flipped, *images, factor)
    weighted = pl.pallas_call(
        final_kernel,
        out_shape=jax.ShapeDtypeStruct((REFS // 2, 2, COLS // 2), jnp.float32),
        in_specs=[VMEM, ANY],
        out_specs=VMEM,
        scratch_shapes=[
            pltpu.VMEM((REFS // 2, COLS), jnp.float32),
            pltpu.SemaphoreType.DMA((4,)),
        ],
        compiler_params=pltpu.CompilerParams(vmem_limit_bytes=16 << 20),
        name="both_groups",
    )(mine, other)
    return weighted, norms.reshape(ROWS)


def shards(references, images, noise_var, shell_of, kept_blocks):
    z, x = lax.axis_index("z"), lax.axis_index("x")
    d, y = lax.axis_index("dom"), lax.axis_index("shell")
    kept = kept_blocks.reshape(MOST)

    shells = jnp.arange(noise_var.shape[0], dtype=jnp.int32)
    picked = jnp.where(shells[:, None] == shell_of[None, :], noise_var[:, None], 0.0)
    weight = 1.0 / jnp.sum(picked, axis=0)
    weight = jnp.concatenate([weight, weight])

    def norm_of(flat):
        return 0.5 * jnp.sum(weight * jnp.square(flat.astype(jnp.float32)), axis=1)[None, :]

    near, far = y ^ 1, 3 - y
    across = 3 - near
    to_near = [(0, 1), (1, 0), (2, 3), (3, 2)]
    to_far = [(0, 3), (3, 0), (1, 2), (2, 1)]
    to_across = [(0, 2), (2, 0), (1, 3), (3, 1)]

    offsets = [b for order in (ORDER_A, ORDER_B) * 2 for piece in order for b in piece]
    offsets = jnp.array(offsets + [(0, 0)] * 15, jnp.int32)
    block = (z + offsets[:, 0]) % NZ * NX + (x + offsets[:, 1]) % NX
    index = jnp.arange(4 * BLOCKS + 15, dtype=jnp.int32)
    slots = jnp.arange(MOST, dtype=jnp.int32)
    slot = jnp.max(jnp.where(kept[None, :] == block[:, None], slots[None, :], -1), axis=1)
    rank = index - 4 * BLOCKS - 2
    tab = jnp.where(rank == y, 0, jnp.where(rank == far, 1, jnp.where(rank == near, 2, 3)))
    for at, value in enumerate(
        (y, far, near, across, y, near, far, across, z * NX + x)
    ):
        tab = jnp.where(rank == NY + at, value, tab)
    tab = jnp.where(rank == -1, d * 256, jnp.where(rank == -2, (1 - d) * 256, tab))
    tab = jnp.where(index < 2 * BLOCKS, slot, jnp.where(index < 4 * BLOCKS, block, tab))

    img = images.reshape(ROWS, COLS)
    early, early_images, pieces_a, pieces_b, refs, norm, tab = gather(
        img[:HALF], img[HALF:], references.reshape(REFS, COLS), norm_of, weight[None, :], tab
    )
    weight = weight[None, :]

    def summed(k, pieces, early, first, second):
        send, keep0, keep1, whole = partial_scores(k, tab, refs, weight, norm, pieces, early)
        got = lax.ppermute(send, "shell", first)
        last = lax.ppermute(keep1 + got[QUARTER:], "shell", second)
        return (keep0, got, last), whole

    sum_a, whole_a = summed(0, pieces_a, (early,), to_near, to_far)
    sum_b, whole_b = summed(1, pieces_b, (), to_far, to_near)

    probs, stats = local_stats(kept, sum_a, sum_b)

    from_near = lax.ppermute(probs, "shell", to_near)
    from_far = lax.ppermute(probs, "shell", to_far)
    top, low = halves(from_far, from_near)
    across_top = lax.ppermute(top, "shell", to_near)
    across_low = lax.ppermute(low, "shell", to_far)
    everyone = lax.all_to_all(
        stats, ("z", "x"), 0, 0, tiled=True
    )
    scale = combine(everyone, stats)
    scales = [scale] + [lax.ppermute(scale, "shell", to) for to in (to_far, to_near, to_across)]
    return weighted_sums(
        tab,
        scales,
        (probs, from_far, from_near, across_top, across_low),
        (early_images, whole_a, whole_b),
    )


def solution(mesh):
    wide = Mesh(mesh.devices.reshape(NZ, NX, 2, NY), ("z", "x", "dom", "shell"))
    orient = ("z", "x")
    placed = (
        P(orient, None, "shell"),
        P(("z", "x", "dom"), None, "shell"),
        P(),
        P("shell"),
        P(orient, "dom", None),
    )
    return jax.shard_map(
        shards,
        mesh=wide,
        in_specs=placed,
        out_specs=(P(("z", "x", "dom"), None, "shell"), P(("z", "x", "dom"))),
        check_vma=False,
    )
```
